256 devices in a mesh: dp: 64 (over z, x, core), mp: 4 (over y).
Axes of the slice: x: 4, y: 4, z: 8, core: 2. Of those that a mesh axis runs over, the one named last changes fastest.
Arguments:
- tokens: bfloat16 [32768, 8192], P('dp', 'mp'), may hold values from -6 to 6
- out_grads: bfloat16 [32768, 28672], P('dp', 'mp'), may hold values from -6 to 6
- test_matrix: bfloat16 [28672, 80], P('mp'), may hold values from -0.03125 to 0.03125
- slot_counts: int32 [64], P('dp'), may hold values from 1 to 512, 16384 in all
Outputs:
- adapter_down: float32 [8192, 80], P(('mp', 'dp'))
- adapter_up: float32 [28672, 80], P(('mp', 'dp'))
The draws below stay inside these ranges and needn't reach their ends.
Inputs may be any that keep to these rules, and one draw needn't show every extreme that they name: `slot_counts`: live slots of each block of 512 rows come first; some block is full.
All inputs are finite; a program needn't handle non-finite values.
Results may differ from the reference program's by a relative error of at most 0.009.
Values may be sent and summed in bfloat16 or wider, within the bound.
No kernel may reach another device: no remote copies, remote signals or barrier semaphores. Data moves between devices by JAX's collectives and lax.ppermute only.
A program may use at most 64 MiB of HBM per device.

```python
import math
import jax
import jax.numpy as jnp
import numpy as np
from jax import lax

D = 8192
FF = 28672
K = 80
TOK_DEV = 512
TOKENS = 32768
N_DP = 64


def normal_field(key, rows, cols):
    return jnp.clip(jax.random.normal(key, (rows, cols), jnp.float32), -6.0, 6.0)


def column_rise(cols, slope):
    where_col = jnp.arange(cols, dtype=jnp.float32) / cols
    return jnp.exp(slope * (where_col - 0.5))[None, :]


def draw_tokens(key, part):
    key = jax.random.fold_in(key, 11)
    values = normal_field(key, TOKENS, D) * column_rise(D, 1.5)
    return jnp.clip(values, -6.0, 6.0).astype(jnp.bfloat16)


def draw_out_grads(key, part):
    key = jax.random.fold_in(key, 23)
    values = normal_field(key, TOKENS, FF)
    return values.astype(jnp.bfloat16)


def level_of(key, extent, cuts, least, largest):
    factor_of = 1.0
    for axis_at, parts in cuts:
        draws = jax.random.uniform(jax.random.fold_in(jax.random.fold_in(key, 6), axis_at), (parts,), jnp.float32, least / len(cuts), largest / len(cuts))
        factor_of = factor_of * jnp.repeat(jnp.exp(draws), extent[axis_at] // parts).reshape((-1,) + (1,) * (len(extent) - 1 - axis_at))
    return factor_of


def split_up(amount, total, most, skew):
    loads = [(1 << 20) // math.isqrt(rank ** skew) + 1 for rank in range(2, amount + 1)]
    spare, holding = total - most - (amount - 1), [1] * (amount - 1)
    while spare > 0:
        candidates = [i for i in range(amount - 1) if holding[i] < most]
        pool, remaining = sum([loads[i] for i in candidates]), spare
        for i in candidates:
            more = min(most - holding[i], max(1, remaining * loads[i] // pool), spare)
            holding[i] = holding[i] + more
            spare = spare - more
    return np.array([most] + holding)


def ragged(own_key, count, total, most, lean):
    if count == 2:
        one = jax.random.randint(own_key, (), max(1, total - most), min(most, total - 1) + 1)
        return jnp.stack([one, total - one])
    lengths = jnp.asarray(split_up(count, total, most, lean), jnp.int32)
    pairs = (count - 1) // 2
    giver, receiver = lengths[1:1 + 2 * pairs:2], lengths[2:2 + 2 * pairs:2]
    margin = jnp.minimum(giver - 1, most - receiver)
    passed = jax.random.randint(jax.random.fold_in(own_key, 1), (pairs,), 0, 1 << 20) % (margin + 1)
    lengths = lengths.at[1:1 + 2 * pairs:2].set(giver - passed).at[2:2 + 2 * pairs:2].set(receiver + passed)
    return lengths[jax.random.permutation(jax.random.fold_in(own_key, 2), count)]


def normal_values(stream_key, dims, scale, most, cuts=(), kind=jnp.bfloat16):
    entries = jax.random.normal(stream_key, dims, jnp.float32) * scale
    if len(cuts) > 0:
        entries = level_of(stream_key, dims, cuts, -0.22, 0.18) * entries
    return jnp.clip(entries, min=-most, max=most).astype(kind)


def setup_inputs(seed: int = 0) -> dict:
    key_list = jax.random.split(jax.random.key(seed), 5)
    return {
        "tokens": draw_tokens(jax.random.fold_in(key_list[4], 71), 0),
        "out_grads": draw_out_grads(jax.random.fold_in(key_list[4], 71), 0),
        "test_matrix": normal_values(key_list[2], (FF, K), FF ** -0.5, 0.03125, ((0, 4),)),
        "slot_counts": ragged(key_list[3], N_DP, N_DP * TOK_DEV // 2, TOK_DEV, 2).astype(jnp.int32),
    }


def contract_tokens(left, right):
    return lax.dot_general(left.astype(jnp.float32), right.astype(jnp.float32), (((0,), (0,)), ((), ())), preferred_element_type=jnp.float32)

def reference(tokens, out_grads, test_matrix, slot_counts):
    live_total = jnp.sum(slot_counts.astype(jnp.float32))
    inv_root = lax.rsqrt(live_total)
    slot_index = jnp.arange(TOKENS, dtype=jnp.int32) % TOK_DEV
    owner_index = jnp.arange(TOKENS, dtype=jnp.int32) // TOK_DEV
    kept_mask = slot_index < slot_counts[owner_index]
    masked = jnp.where(kept_mask[:, None], tokens, jnp.zeros_like(tokens))
    sketch = jnp.dot(out_grads.astype(jnp.float32), test_matrix.astype(jnp.float32), preferred_element_type=jnp.float32).astype(jnp.bfloat16)
    ranged = (inv_root * contract_tokens(masked, sketch)).astype(jnp.bfloat16)
    back = (jnp.dot(masked.astype(jnp.float32), ranged.astype(jnp.float32), preferred_element_type=jnp.float32) * D ** (-0.5)).astype(jnp.bfloat16)
    transposed = (inv_root * contract_tokens(out_grads, back)).astype(jnp.bfloat16)
    again = (jnp.dot(out_grads.astype(jnp.float32), transposed.astype(jnp.float32), preferred_element_type=jnp.float32) * FF ** (-0.5)).astype(jnp.bfloat16)
    whole_range = inv_root * contract_tokens(masked, again)
    gram = jnp.dot(whole_range.T, whole_range, precision=lax.Precision.HIGHEST)
    lower = jnp.linalg.cholesky(gram)
    basis = lax.linalg.triangular_solve(lower, whole_range, left_side=False, lower=True, transpose_a=True)
    adapter_down = basis * D ** 0.5
    projected = jnp.dot(masked.astype(jnp.float32), basis.astype(jnp.bfloat16).astype(jnp.float32), preferred_element_type=jnp.float32).astype(jnp.bfloat16)
    adapter_up = inv_root * contract_tokens(out_grads, projected)
    return (adapter_down, adapter_up)
```

```python
import jax
import jax.numpy as jnp
from jax import lax
from jax.sharding import Mesh, PartitionSpec as P

D = 8192
FF = 28672
K = 80
LIVE = 16384
F32 = jnp.float32
BF16 = jnp.bfloat16


def dot(left, right, contract):
    return lax.dot_general(left, right, (contract, ((), ())), preferred_element_type=F32)


def along_features(small, big):
    return dot(small, big, ((1,), (1,)))


def along_tokens(small, big):
    return dot(small, big, ((1,), (0,)))


def shifted(value, axis, size, step):
    return lax.ppermute(value, axis, [(i, (i + step) % size) for i in range(size)])


def y_sum(part):
    sent = part.astype(BF16)
    came = [shifted(sent, "y", 4, step) for step in (1, 2, 3)]
    total = sent.astype(F32)
    for piece in came:
        total = total + piece.astype(F32)
    return total


def to_tiles(array):
    rows, cols = array.shape
    tiles = array.reshape(rows // 8, 8, cols // 128, 128).transpose(0, 2, 1, 3)
    return tiles.reshape(-1, 8, 128)


def from_tiles(tiles, rows, cols):
    split = tiles.reshape(rows // 8, cols // 128, 8, 128).transpose(0, 2, 1, 3)
    return split.reshape(rows, cols)


def exchange(pieces, axes):
    return lax.all_to_all(pieces, axes, 0, 0, tiled=True)


def spread(piece, axes, count):
    return exchange(jnp.broadcast_to(piece[None], (count,) + piece.shape), axes)


def dp_sum_small(part, scale):
    rows, cols = part.shape
    pieces = to_tiles(part.astype(BF16)).reshape(8, -1, 8, 128)
    mine = exchange(pieces, ("x", "c")).astype(F32).sum(0).astype(BF16)
    mine = (spread(mine, "z", 8).astype(F32).sum(0) * scale).astype(BF16)
    whole = spread(mine, ("x", "c"), 8)
    return from_tiles(whole, rows, cols)


def core_scatter(halves):
    core = lax.axis_index("c")
    kept = lax.dynamic_index_in_dim(halves, core, 0, keepdims=False)
    sent = lax.dynamic_index_in_dim(halves, 1 - core, 0, keepdims=False)
    came = shifted(sent, "c", 2, 1)
    return (kept.astype(F32) + came.astype(F32)).astype(BF16)


def core_gather(half):
    other = shifted(half, "c", 2, 1)
    first = lax.axis_index("c") == 0
    return jnp.stack([jnp.where(first, half, other), jnp.where(first, other, half)])


def dp_sum_big(part, scale):
    rows, cols = part.shape
    tiles = to_tiles(part.astype(BF16))
    count = tiles.shape[0]
    per = -(-count // 64)
    tiles = jnp.pad(tiles, ((0, 64 * per - count), (0, 0), (0, 0)))
    half = core_scatter(tiles.reshape(2, 32, per, 8, 128))
    mine = (exchange(half, ("z", "x")).astype(F32).sum(0) * scale).astype(BF16)
    whole = core_gather(spread(mine, ("z", "x"), 32))
    return from_tiles(whole.reshape(64 * per, 8, 128)[:count], rows, cols)


def local(tokens, out_grads, test_matrix, slot_counts):
    rows = tokens.shape[0]
    live_rows = slot_counts[0]
    kept = (jnp.arange(rows, dtype=jnp.int32) < live_rows)[None, :]
    scale = LIVE ** -0.5

    def masked(value):
        return jnp.where(kept, value, 0.0).astype(BF16)

    sketch = masked(y_sum(dot(test_matrix, out_grads, ((0,), (1,)))))
    ranged = dp_sum_small(along_tokens(sketch, tokens), scale)
    back = masked(y_sum(along_features(ranged, tokens)) * D ** -0.5)
    transposed = dp_sum_big(along_tokens(back, out_grads), scale)
    again = masked(y_sum(along_features(transposed, out_grads)) * FF ** -0.5)
    whole_range = dp_sum_small(along_tokens(again, tokens), scale)

    gram_part = along_features(whole_range, whole_range)
    gram = gram_part
    for step in (1, 2, 3):
        gram = gram + shifted(gram_part, "y", 4, step)
    lower = jnp.linalg.cholesky(gram)
    inverse = lax.linalg.triangular_solve(
        lower, jnp.eye(K, dtype=F32), left_side=True, lower=True
    )

    projected = masked(y_sum(along_features(whole_range, tokens)))
    up_part = along_tokens(projected, out_grads).astype(BF16)
    owned = up_part.shape[1] // 64
    up_part = up_part.reshape(K, 32, 2, owned).transpose(2, 1, 0, 3)
    digits = jnp.stack([live_rows // 32, live_rows % 32]).astype(BF16)
    digits = jnp.broadcast_to(digits, (2, 32, K, 2))
    up_part = jnp.concatenate([up_part, digits], axis=3)
    up_sum = exchange(core_scatter(up_part), ("z", "x")).astype(F32).sum(0)
    live_total = 32.0 * up_sum[0, owned] + up_sum[0, owned + 1]
    inv_root = lax.rsqrt(live_total)
    adapter_up = inv_root * jnp.dot(
        inverse, up_sum[:, :owned], precision=lax.Precision.HIGHEST
    ).T

    place = lax.axis_index(("z", "x", "c"))
    width = whole_range.shape[1] // 64
    own = lax.dynamic_slice_in_dim(whole_range, place * width, width, 1).astype(F32)
    adapter_down = jnp.dot(inverse, own, precision=lax.Precision.HIGHEST).T * D ** 0.5
    return adapter_down, adapter_up


def solution(mesh):
    split = Mesh(mesh.devices.reshape(8, 4, 2, 4), ("z", "x", "c", "y"))
    dp = ("z", "x", "c")
    placed = (P(dp, "y"), P(dp, "y"), P("y", None), P(dp))
    return jax.shard_map(
        local,
        mesh=split,
        in_specs=placed,
        out_specs=(P(("y",) + dp, None), P(("y",) + dp, None)),
        check_vma=False,
    )
```

```python
import functools

import jax
import jax.numpy as jnp
from jax import lax
from jax.experimental import pallas as pl
from jax.experimental.pallas import tpu as pltpu
from jax.sharding import Mesh, PartitionSpec as P

D = 8192
FF = 28672
K = 80
LIVE = 16384
F32 = jnp.float32
BF16 = jnp.bfloat16


def dot(left, right, contract):
    return lax.dot_general(left, right, (contract, ((), ())), preferred_element_type=F32)


def along_features(small, big):
    return dot(small, big, ((1,), (1,)))


def along_tokens(small, big):
    return dot(small, big, ((1,), (0,)))


def shifted(value, axis, size, step):
    return lax.ppermute(value, axis, [(i, (i + step) % size) for i in range(size)])


def y_pieces(part):
    sent = part.astype(BF16)
    return [sent] + [shifted(sent, "y", 4, step) for step in (1, 2, 3)]


def y_sum(part):
    pieces = y_pieces(part)
    total = pieces[0].astype(F32)
    for piece in pieces[1:]:
        total = total + piece.astype(F32)
    return total


def to_tiles(array):
    rows, cols = array.shape
    tiles = array.reshape(rows // 8, 8, cols // 128, 128).transpose(0, 2, 1, 3)
    return tiles.reshape(-1, 8, 128)


def from_tiles(tiles, rows, cols):
    split = tiles.reshape(rows // 8, cols // 128, 8, 128).transpose(0, 2, 1, 3)
    return split.reshape(rows, cols)


def aligned(square):
    return jnp.pad(square, ((0, 0), (0, 128 - square.shape[1])))


def exchange(pieces, axes):
    return lax.all_to_all(pieces, axes, 0, 0, tiled=True)


def spread(piece, axes, count):
    return exchange(jnp.broadcast_to(piece[None], (count,) + piece.shape), axes)


def core_add(kept, sent):
    came = shifted(sent, "c", 2, 1)
    return (kept.astype(F32) + came.astype(F32)).astype(BF16)


def chip_sum(half, scale):
    rows, cols = half.shape
    tiles = to_tiles(half)
    count = tiles.shape[0]
    per = -(-count // 32)
    tiles = jnp.pad(tiles, ((0, 32 * per - count), (0, 0), (0, 0)))
    pieces = tiles.reshape(32, per, 8, 128)
    mine = (exchange(pieces, ("z", "x")).astype(F32).sum(0) * scale).astype(BF16)
    whole = spread(mine, ("z", "x"), 32).reshape(32 * per, 8, 128)[:count]
    own = from_tiles(whole, rows, cols)
    return jnp.concatenate([own, shifted(own, "c", 2, 1)], 0)


CHUNKS = 14
BLOCK = 1024
VMEM = pl.BlockSpec(memory_space=pltpu.VMEM)
SMEM = pl.BlockSpec(memory_space=pltpu.SMEM)


def cost(grads):
    rows, cols = grads.shape
    return pl.CostEstimate(
        flops=2 * K * rows * cols, bytes_accessed=2 * rows * cols, transcendentals=0
    )


PARAMS = pltpu.CompilerParams(vmem_limit_bytes=16 << 20)


def load_kernel(
    place_ref, test_ref, grads_ref, part_ref, held_ref, test_held, sems, test_sems
):
    width = grads_ref.shape[1] // CHUNKS
    copies = []
    for k in range(CHUNKS):
        cols = pl.ds(k * width, width)
        first = pltpu.make_async_copy(
            test_ref.at[:, cols], test_held.at[:, cols], test_sems.at[k]
        )
        second = pltpu.make_async_copy(
            grads_ref.at[:, cols], held_ref.at[:, cols], sems.at[k]
        )
        first.start()
        second.start()
        copies.append((first, second))
    total = None
    for k in range(CHUNKS):
        cols = pl.ds(k * width, width)
        copies[k][0].wait()
        copies[k][1].wait()
        step = dot(test_held[:, cols], held_ref[:, cols], ((1,), (1,)))
        total = step if total is None else total + step
    swapped = jnp.concatenate([total[K // 2 :], total[: K // 2]], 0)
    part_ref[...] = jnp.where(place_ref[1] == 0, total, swapped).astype(BF16)


def load_and_sketch(place, test_t, grads):
    rows, cols = grads.shape
    test_t = pltpu.with_memory_space_constraint(test_t, pltpu.HBM)
    grads = pltpu.with_memory_space_constraint(grads, pltpu.HBM)
    return pl.pallas_call(
        load_kernel,
        out_shape=(
            jax.ShapeDtypeStruct((K, rows), BF16),
            pltpu.VMEM((rows, cols), BF16),
        ),
        in_specs=[SMEM] + [pl.BlockSpec(memory_space=pl.ANY)] * 2,
        out_specs=(VMEM, VMEM),
        scratch_shapes=[
            pltpu.VMEM((K, cols), BF16),
            pltpu.SemaphoreType.DMA((CHUNKS,)),
            pltpu.SemaphoreType.DMA((CHUNKS,)),
        ],
        compiler_params=PARAMS,
        cost_estimate=cost(grads),
        name="load_and_sketch",
    )(place, test_t, grads)


def summed_small(live_ref, refs, scale):
    total = refs[0][...].astype(F32)
    for ref in refs[1:]:
        total = total + ref[...].astype(F32)
    row = lax.broadcasted_iota(jnp.int32, total.shape, 1)
    return jnp.where(row < live_ref[0], total * scale, 0.0).astype(BF16)


def token_kernel(scale, live_ref, *refs):
    big_ref, kept_ref, sent_ref = refs[-3:]
    small = summed_small(live_ref, refs[:-3], scale)
    half = K // 2
    for k in range(big_ref.shape[1] // BLOCK):
        cols = slice(k * BLOCK, (k + 1) * BLOCK)
        out = dot(small, big_ref[:, cols], ((1,), (0,)))
        kept_ref[:, cols] = out[:half].astype(kept_ref.dtype)
        sent_ref[:, cols] = out[half:].astype(sent_ref.dtype)


def token_parts(live, pieces, big, scale, dtype):
    big = pltpu.with_memory_space_constraint(big, pltpu.VMEM)
    shape = jax.ShapeDtypeStruct((K // 2, big.shape[1]), dtype)
    return pl.pallas_call(
        functools.partial(token_kernel, scale),
        out_shape=(shape, shape),
        in_specs=[SMEM] + [VMEM] * (len(pieces) + 1),
        out_specs=(VMEM, VMEM),
        compiler_params=PARAMS,
        cost_estimate=cost(big),
        name="token_parts",
    )(live, *pieces, big)


def again_kernel(small_ref, big_ref, part_ref):
    total = None
    for k in range(big_ref.shape[1] // BLOCK):
        cols = slice(k * BLOCK, (k + 1) * BLOCK)
        step = dot(small_ref[:, cols], big_ref[:, cols], ((1,), (1,)))
        total = step if total is None else total + step
    part_ref[...] = total.astype(BF16)


def again_part(small, held):
    rows, cols = held.shape
    held = pltpu.with_memory_space_constraint(held, pltpu.VMEM)
    return pl.pallas_call(
        again_kernel,
        out_shape=jax.ShapeDtypeStruct((K, rows), BF16),
        in_specs=[VMEM, VMEM],
        out_specs=VMEM,
        compiler_params=PARAMS,
        cost_estimate=cost(held),
        name="again_part",
    )(small, held)


def up_kernel(place_ref, live_ref, small_ref, big_ref, kept_ref, sent_ref):
    owned = big_ref.shape[1] // 64
    lane = lax.broadcasted_iota(jnp.int32, (K, 128), 1)
    live = live_ref[0]
    high = (live // 32).astype(F32)
    low = (live % 32).astype(F32)
    digits = jnp.where(lane == owned, high, jnp.where(lane == owned + 1, low, 0.0))
    tail = digits.astype(BF16)[:, owned:]
    wide = small_ref[...].astype(F32)
    both = jnp.concatenate([wide, wide[: K // 2]], 0).astype(BF16)

    def fill(places):
        for z in range(8):
            block = big_ref[:, z * 8 * owned : (z + 1) * 8 * owned]
            out = dot(both, block, ((1,), (0,)))
            views = (out[:K].astype(BF16), out[K // 2 :].astype(BF16))
            for x in range(4):
                for c in range(2):
                    at = (2 * x + c) * owned
                    ref, turn = places[c]
                    piece = views[turn][:, at : at + owned]
                    ref[4 * z + x] = jnp.concatenate([piece, tail], 1)

    @pl.when(place_ref[1] == 0)
    def _():
        fill(((kept_ref, 0), (sent_ref, 1)))

    @pl.when(place_ref[1] != 0)
    def _():
        fill(((sent_ref, 1), (kept_ref, 0)))


def up_parts(place, live, small, held):
    held = pltpu.with_memory_space_constraint(held, pltpu.VMEM)
    shape = jax.ShapeDtypeStruct((32, K, 128), BF16)
    return pl.pallas_call(
        up_kernel,
        out_shape=(shape, shape),
        in_specs=[SMEM] * 2 + [VMEM] * 2,
        out_specs=(VMEM, VMEM),
        compiler_params=PARAMS,
        cost_estimate=cost(held),
        name="up_parts",
    )(place, live, small, held)


def unturned(rows, first):
    return jnp.where(first, rows, jnp.roll(rows, K // 2, 0))


def local(tokens, out_grads, test_matrix, slot_counts):
    rows = tokens.shape[0]
    live_rows = slot_counts[0]
    kept = (jnp.arange(rows, dtype=jnp.int32) < live_rows)[None, :]
    scale = LIVE ** -0.5
    place = jnp.stack([lax.axis_index(("z", "x", "c")), lax.axis_index("c")])
    width = tokens.shape[1] // 64

    def masked(value):
        return jnp.where(kept, value, 0.0).astype(BF16)

    sketch_part, held = load_and_sketch(place, test_matrix.T, out_grads)
    sketch_pieces = y_pieces(sketch_part)
    ranged = chip_sum(
        core_add(*token_parts(slot_counts, sketch_pieces, tokens, 1.0, F32)), scale
    )
    back_pieces = y_pieces(along_features(ranged, tokens))
    transposed = chip_sum(
        core_add(*token_parts(slot_counts, back_pieces, held, D ** -0.5, BF16)), scale
    )
    again_pieces = y_pieces(again_part(transposed, held))
    whole_range = chip_sum(
        core_add(*token_parts(slot_counts, again_pieces, tokens, FF ** -0.5, F32)), scale
    )

    gram_part = along_features(whole_range, whole_range)
    high = gram_part.astype(BF16)
    low = (gram_part - high.astype(F32)).astype(BF16)
    joined = jnp.concatenate(
        [along_features(whole_range, tokens).astype(BF16), aligned(high), aligned(low)], 1
    )
    summed = y_sum(joined)
    projected = masked(summed[:, :rows])
    gram = summed[:, rows : rows + K] + summed[:, rows + 128 : rows + 128 + K]
    kept_up, sent_up = up_parts(place, slot_counts, projected, held)
    gram, sent_up, place = lax.optimization_barrier((gram, sent_up, place))
    first = place[1] == 0
    gram = unturned(unturned(gram, first).T, first)
    lower = jnp.linalg.cholesky(gram)
    inverse = lax.linalg.triangular_solve(
        lower, jnp.eye(K, dtype=F32), left_side=True, lower=True
    )

    up_sum = exchange(core_add(kept_up, sent_up), ("z", "x")).astype(F32).sum(0)
    owned = out_grads.shape[1] // 64
    live_total = 32.0 * up_sum[0, owned] + up_sum[0, owned + 1]
    inv_root = lax.rsqrt(live_total)
    adapter_up = inv_root * jnp.dot(
        inverse, unturned(up_sum[:, :owned], first), precision=lax.Precision.HIGHEST
    ).T

    own = lax.dynamic_slice_in_dim(whole_range, place[0] * width, width, 1)
    own = unturned(own.astype(F32), first)
    adapter_down = jnp.dot(inverse, own, precision=lax.Precision.HIGHEST).T * D ** 0.5
    return adapter_down, adapter_up


def solution(mesh):
    split = Mesh(mesh.devices.reshape(8, 4, 2, 4), ("z", "x", "c", "y"))
    dp = ("z", "x", "c")
    placed = (P(dp, "y"), P(dp, "y"), P("y", None), P(dp))
    return jax.shard_map(
        local,
        mesh=split,
        in_specs=placed,
        out_specs=(P(("y",) + dp, None), P(("y",) + dp, None)),
        check_vma=False,
    )
```

```python
import functools

import jax
import jax.numpy as jnp
from jax import lax
from jax.experimental import pallas as pl
from jax.experimental.pallas import tpu as pltpu
from jax.sharding import Mesh, PartitionSpec as P

D = 8192
FF = 28672
K = 80
HALF = K // 2
LIVE = 16384
F32 = jnp.float32
BF16 = jnp.bfloat16
CHUNKS = 14
BLOCK = 1024
HOLDS = 8
VMEM = pl.BlockSpec(memory_space=pltpu.VMEM)
SMEM = pl.BlockSpec(memory_space=pltpu.SMEM)
PARAMS = pltpu.CompilerParams(vmem_limit_bytes=16 << 20)


def dot(left, right, contract):
    return lax.dot_general(left, right, (contract, ((), ())), preferred_element_type=F32)


def shifted(value, axis, size, step):
    return lax.ppermute(value, axis, [(i, (i + step) % size) for i in range(size)])


def sibling(value):
    return shifted(value, "c", 2, 1)


def y_pieces(sent):
    return [sent] + [shifted(sent, "y", 4, step) for step in (1, 2, 3)]


def to_tiles(array):
    rows, cols = array.shape
    tiles = array.reshape(rows // 8, 8, cols // 128, 128).transpose(0, 2, 1, 3)
    return tiles.reshape(-1, 8, 128)


def from_tiles(tiles, rows, cols):
    split = tiles.reshape(rows // 8, cols // 128, 8, 128).transpose(0, 2, 1, 3)
    return split.reshape(rows, cols)


def exchange(pieces, axes):
    return lax.all_to_all(pieces, axes, 0, 0, tiled=True)


def spread(piece, axes, count):
    return exchange(jnp.broadcast_to(piece[None], (count,) + piece.shape), axes)


def chips_sum(part, scale):
    rows, cols = part.shape
    tiles = to_tiles(part)
    count = tiles.shape[0]
    per = -(-count // 32)
    tiles = jnp.pad(tiles, ((0, 32 * per - count), (0, 0), (0, 0)))
    pieces = tiles.reshape(32, per, 8, 128)
    mine = (exchange(pieces, ("z", "x")).astype(F32).sum(0) * scale).astype(BF16)
    whole = spread(mine, ("z", "x"), 32).reshape(32 * per, 8, 128)[:count]
    return from_tiles(whole, rows, cols)


def cost(big):
    rows, cols = big.shape
    return pl.CostEstimate(
        flops=4 * HALF * rows * cols, bytes_accessed=4 * rows * cols, transcendentals=0
    )


def in_vmem(array):
    return pltpu.with_memory_space_constraint(array, pltpu.VMEM)


def hold_kernel(given_ref, held_ref, sems):
    rows = given_ref.shape[0] // HOLDS
    copies = []
    for k in range(HOLDS):
        part = pl.ds(k * rows, rows)
        copy = pltpu.make_async_copy(given_ref.at[part], held_ref.at[part], sems.at[k])
        copy.start()
        copies.append(copy)
    for copy in copies:
        copy.wait()


def hold(given):
    given = pltpu.with_memory_space_constraint(given, pltpu.HBM)
    return pl.pallas_call(
        hold_kernel,
        out_shape=pltpu.VMEM(given.shape, given.dtype),
        in_specs=[pl.BlockSpec(memory_space=pl.ANY)],
        out_specs=VMEM,
        scratch_shapes=[pltpu.SemaphoreType.DMA((HOLDS,))],
        compiler_params=PARAMS,
        cost_estimate=pl.CostEstimate(
            flops=0, bytes_accessed=4 * given.size, transcendentals=0
        ),
        name="hold",
    )(given)


def load_kernel(
    place_ref, test_ref, grads_ref, kept_ref, sent_ref, held_ref, test_held, sems, test_sems
):
    width = grads_ref.shape[1] // CHUNKS
    copies = []
    for k in range(CHUNKS):
        cols = pl.ds(k * width, width)
        first = pltpu.make_async_copy(
            test_ref.at[:, cols], test_held.at[:, cols], test_sems.at[k]
        )
        second = pltpu.make_async_copy(
            grads_ref.at[:, cols], held_ref.at[:, cols], sems.at[k]
        )
        first.start()
        second.start()
        copies.append((first, second))
    total = None
    for k in range(CHUNKS):
        cols = pl.ds(k * width, width)
        copies[k][0].wait()
        copies[k][1].wait()
        step = dot(test_held[:, cols], held_ref[:, cols], ((1,), (1,)))
        total = step if total is None else total + step
    first = place_ref[1] == 0
    kept_ref[...] = jnp.where(first, total[:HALF], total[HALF:]).astype(BF16)
    sent_ref[...] = jnp.where(first, total[HALF:], total[:HALF]).astype(BF16)


def load_and_sketch(place, test_t, grads):
    rows, cols = grads.shape
    test_t = pltpu.with_memory_space_constraint(test_t, pltpu.HBM)
    grads = pltpu.with_memory_space_constraint(grads, pltpu.HBM)
    part = jax.ShapeDtypeStruct((HALF, rows), BF16)
    return pl.pallas_call(
        load_kernel,
        out_shape=(part, part, pltpu.VMEM((rows, cols), BF16)),
        in_specs=[SMEM] + [pl.BlockSpec(memory_space=pl.ANY)] * 2,
        out_specs=(VMEM,) * 3,
        scratch_shapes=[
            pltpu.VMEM((K, cols), BF16),
            pltpu.SemaphoreType.DMA((CHUNKS,)),
            pltpu.SemaphoreType.DMA((CHUNKS,)),
        ],
        compiler_params=PARAMS,
        cost_estimate=cost(grads),
        name="load_and_sketch",
    )(place, test_t, grads)


def summed_small(place_ref, refs, scale):
    total = refs[0][...].astype(F32)
    for ref in refs[1:]:
        total = total + ref[...].astype(F32)
    rows = total.shape[1] // 2
    slot = lax.broadcasted_iota(jnp.int32, total.shape, 1)
    own = slot < place_ref[2]
    other = (slot >= rows) & (slot < place_ref[3] + rows)
    return jnp.where(own | other, total * scale, 0.0).astype(BF16)


def token_kernel(scale, place_ref, *refs):
    own_ref, other_ref, part_ref = refs[-3:]
    small = summed_small(place_ref, refs[:-3], scale)
    rows = own_ref.shape[0]
    for k in range(own_ref.shape[1] // BLOCK):
        cols = slice(k * BLOCK, (k + 1) * BLOCK)
        out = dot(small[:, :rows], own_ref[:, cols], ((1,), (0,)))
        out = out + dot(small[:, rows:], other_ref[:, cols], ((1,), (0,)))
        part_ref[:, cols] = out.astype(BF16)


def token_part(place, pieces, own, other, scale):
    return pl.pallas_call(
        functools.partial(token_kernel, scale),
        out_shape=jax.ShapeDtypeStruct((HALF, own.shape[1]), BF16),
        in_specs=[SMEM] + [VMEM] * (len(pieces) + 2),
        out_specs=VMEM,
        compiler_params=PARAMS,
        cost_estimate=cost(own),
        name="token_part",
    )(place, *pieces, in_vmem(own), in_vmem(other))


def feature_kernel(small_ref, own_ref, other_ref, part_ref):
    rows = own_ref.shape[0]
    for at, big_ref in ((0, own_ref), (rows, other_ref)):
        total = None
        for k in range(big_ref.shape[1] // BLOCK):
            cols = slice(k * BLOCK, (k + 1) * BLOCK)
            step = dot(small_ref[:, cols], big_ref[:, cols], ((1,), (1,)))
            total = step if total is None else total + step
        part_ref[:, at : at + rows] = total.astype(BF16)


def feature_part(small, own, other):
    return pl.pallas_call(
        feature_kernel,
        out_shape=jax.ShapeDtypeStruct((HALF, 2 * own.shape[0]), BF16),
        in_specs=[VMEM] * 3,
        out_specs=VMEM,
        compiler_params=PARAMS,
        cost_estimate=cost(own),
        name="feature_part",
    )(small, in_vmem(own), in_vmem(other))


def up_kernel(place_ref, *refs):
    own_ref, other_ref, part_ref, gram_ref = refs[-4:]
    rows = own_ref.shape[0]
    pieces = [ref.at[:, : 2 * rows] for ref in refs[:-4]]
    small = summed_small(place_ref, pieces, 1.0)
    gram = None
    for ref in refs[:-4]:
        high = ref[:, 2 * rows : 2 * rows + 128].astype(F32)
        low = ref[:, 2 * rows + 128 : 2 * rows + 256].astype(F32)
        gram = high + low if gram is None else gram + (high + low)
    gram_ref[...] = gram
    width = own_ref.shape[1] // 32
    lane = lax.broadcasted_iota(jnp.int32, (HALF, 256), 1)
    high = (place_ref[2] // 32 + place_ref[3] // 32).astype(F32)
    low = (place_ref[2] % 32 + place_ref[3] % 32).astype(F32)
    digits = jnp.where(lane == width, high, jnp.where(lane == width + 1, low, 0.0))
    tail = digits.astype(BF16)[:, width:]
    for z in range(8):
        cols = slice(4 * z * width, 4 * (z + 1) * width)
        out = dot(small[:, :rows], own_ref[:, cols], ((1,), (0,)))
        out = out + dot(small[:, rows:], other_ref[:, cols], ((1,), (0,)))
        out = out.astype(BF16)
        for x in range(4):
            piece = out[:, x * width : (x + 1) * width]
            part_ref[4 * z + x] = jnp.concatenate([piece, tail], 1)


def up_part(place, pieces, own, other):
    return pl.pallas_call(
        up_kernel,
        out_shape=(
            jax.ShapeDtypeStruct((32, HALF, 256), BF16),
            jax.ShapeDtypeStruct((HALF, 128), F32),
        ),
        in_specs=[SMEM] + [VMEM] * (len(pieces) + 2),
        out_specs=(VMEM, VMEM),
        compiler_params=PARAMS,
        cost_estimate=cost(own),
        name="up_part",
    )(place, *pieces, in_vmem(own), in_vmem(other))


def split_kernel(place_ref, pieces_ref, kept_ref, sent_ref):
    owned = kept_ref.shape[1] - 16
    total = pieces_ref[0].astype(F32)
    for k in range(1, pieces_ref.shape[0]):
        total = total + pieces_ref[k].astype(F32)
    tail = total[:, 2 * owned : 2 * owned + 16]
    first = jnp.concatenate([total[:, :owned], tail], 1)
    second = total[:, owned : 2 * owned + 16]
    mine = place_ref[1] == 0
    kept_ref[...] = jnp.where(mine, first, second)
    sent_ref[...] = jnp.where(mine, second, first)


def split_up(place, pieces, owned):
    shape = jax.ShapeDtypeStruct((HALF, owned + 16), F32)
    return pl.pallas_call(
        split_kernel,
        out_shape=(shape, shape),
        in_specs=[SMEM, VMEM],
        out_specs=(VMEM, VMEM),
        compiler_params=PARAMS,
        name="split_up",
    )(place, pieces)


def finish_kernel(place_ref, kept_ref, came_ref, inverse_ref, up_ref):
    owned = up_ref.shape[1]
    kept, came = kept_ref[...], came_ref[...]
    high, low = kept[:1, owned : owned + 1], kept[:1, owned + 1 : owned + 2]
    inv_root = lax.rsqrt(32.0 * high + low)
    mine = place_ref[1] == 0
    total = jnp.concatenate([jnp.where(mine, kept, came), jnp.where(mine, came, kept)], 0)
    up = lax.dot_general(
        inverse_ref[...],
        total,
        (((1,), (0,)), ((), ())),
        precision=lax.Precision.HIGHEST,
        preferred_element_type=F32,
    )
    up_ref[...] = (inv_root * up)[:, :owned]


def finish_up(place, kept, came, inverse, owned):
    return pl.pallas_call(
        finish_kernel,
        out_shape=jax.ShapeDtypeStruct((K, owned), F32),
        in_specs=[SMEM] + [VMEM] * 3,
        out_specs=VMEM,
        compiler_params=PARAMS,
        name="finish_up",
    )(place, kept, came, inverse)


def both_halves(first, own, other):
    return jnp.where(
        first, jnp.concatenate([own, other], 0), jnp.concatenate([other, own], 0)
    )


def aligned(block):
    return jnp.pad(block, ((0, 0), (0, 128 - block.shape[1])))


def local(tokens, out_grads, test_matrix, slot_counts):
    spots = jnp.stack([lax.axis_index(("z", "x", "c")), lax.axis_index("c")])
    place = jnp.concatenate([spots, slot_counts, sibling(slot_counts)])
    scale = LIVE ** -0.5
    width = tokens.shape[1] // 64

    kept, sent, grads = load_and_sketch(spots, test_matrix.T, out_grads)
    sketch_part = jnp.concatenate([kept, sibling(sent)], 1)
    other_tokens, sketch_part = lax.optimization_barrier((sibling(tokens), sketch_part))
    sent_grads, sketch_part = lax.optimization_barrier((out_grads, sketch_part))
    other_grads = sibling(sent_grads)
    other_tokens = hold(other_tokens)

    ranged = chips_sum(
        token_part(place, y_pieces(sketch_part), tokens, other_tokens, 1.0), scale
    )
    back_part = feature_part(ranged, tokens, other_tokens)
    other_grads, back_part = lax.optimization_barrier((other_grads, back_part))
    back = y_pieces(back_part)
    other_grads = hold(other_grads)
    transposed = chips_sum(
        token_part(place, back, grads, other_grads, D ** -0.5), scale
    )
    again = y_pieces(feature_part(transposed, grads, other_grads))
    whole_range = chips_sum(
        token_part(place, again, tokens, other_tokens, FF ** -0.5), scale
    )

    other_range = sibling(whole_range)
    both = jnp.concatenate([whole_range, other_range], 0)
    gram_part = dot(whole_range, both, ((1,), (1,)))
    high = gram_part.astype(BF16)
    low = (gram_part - high.astype(F32)).astype(BF16)
    projected = feature_part(whole_range, tokens, other_tokens)
    joined = y_pieces(jnp.concatenate([projected, aligned(high), aligned(low)], 1))

    up, gram_rows = up_part(place, joined, grads, other_grads)
    up_pieces = exchange(up, ("z", "x"))
    gram_rows, place = lax.optimization_barrier((gram_rows, place))
    gram_rows = gram_rows[:, :K]
    first = place[1] == 0
    other_rows = sibling(gram_rows)
    other_rows = jnp.roll(other_rows, HALF, 1)
    gram = both_halves(first, gram_rows, other_rows)
    gram = jnp.where(first, gram, jnp.roll(gram, HALF, 1))
    lower = jnp.linalg.cholesky(gram)
    inverse = lax.linalg.triangular_solve(
        lower, jnp.eye(K, dtype=F32), left_side=True, lower=True
    )

    owned = out_grads.shape[1] // 64
    kept_up, sent_up = split_up(place, up_pieces, owned)
    adapter_up = finish_up(place, kept_up, sibling(sent_up), inverse, owned).T

    own = both_halves(first, whole_range, other_range)
    own = lax.dynamic_slice_in_dim(own, place[0] * width, width, 1).astype(F32)
    adapter_down = jnp.dot(inverse, own, precision=lax.Precision.HIGHEST).T * D ** 0.5
    return adapter_down, adapter_up


def solution(mesh):
    split = Mesh(mesh.devices.reshape(8, 4, 2, 4), ("z", "x", "c", "y"))
    dp = ("z", "x", "c")
    placed = (P(dp, "y"), P(dp, "y"), P("y", None), P(dp))
    return jax.shard_map(
        local,
        mesh=split,
        in_specs=placed,
        out_specs=(P(("y",) + dp, None), P(("y",) + dp, None)),
        check_vma=False,
    )
```

```python
import functools

import jax
import jax.numpy as jnp
from jax import lax
from jax.experimental import pallas as pl
from jax.experimental.pallas import tpu as pltpu
from jax.sharding import Mesh, PartitionSpec as P

D = 8192
FF = 28672
K = 80
HALF = K // 2
LIVE = 16384
F32 = jnp.float32
BF16 = jnp.bfloat16
CHUNKS = 14
BLOCK = 1024
HOLDS = 8
VMEM = pl.BlockSpec(memory_space=pltpu.VMEM)
SMEM = pl.BlockSpec(memory_space=pltpu.SMEM)
PARAMS = pltpu.CompilerParams(vmem_limit_bytes=16 << 20)


def dot(left, right, contract):
    return lax.dot_general(left, right, (contract, ((), ())), preferred_element_type=F32)


def shifted(value, axis, size, step):
    return lax.ppermute(value, axis, [(i, (i + step) % size) for i in range(size)])


def sibling(value):
    return shifted(value, "c", 2, 1)


def y_pieces(sent):
    return [sent] + [shifted(sent, "y", 4, step) for step in (3, 2, 1)]


def to_tiles(array):
    rows, cols = array.shape
    tiles = array.reshape(rows // 8, 8, cols // 128, 128).transpose(0, 2, 1, 3)
    return tiles.reshape(-1, 8, 128)


def from_tiles(tiles, rows, cols):
    split = tiles.reshape(rows // 8, cols // 128, 8, 128).transpose(0, 2, 1, 3)
    return split.reshape(rows, cols)


def exchange(pieces, axes):
    return lax.all_to_all(pieces, axes, 0, 0, tiled=True)


def spread(piece, axes, count):
    return exchange(jnp.broadcast_to(piece[None], (count,) + piece.shape), axes)


def chips_sum(part, scale, axes=("z", "x")):
    rows, cols = part.shape
    tiles = to_tiles(part)
    count = tiles.shape[0]
    per = -(-count // 32)
    tiles = jnp.pad(tiles, ((0, 32 * per - count), (0, 0), (0, 0)))
    pieces = tiles.reshape(32, per, 8, 128)
    mine = (exchange(pieces, axes).astype(F32).sum(0) * scale).astype(BF16)
    whole = spread(mine, axes, 32).reshape(32 * per, 8, 128)[:count]
    return from_tiles(whole, rows, cols)


def cost(big):
    rows, cols = big.shape
    return pl.CostEstimate(
        flops=4 * HALF * rows * cols, bytes_accessed=4 * rows * cols, transcendentals=0
    )


def in_vmem(array):
    return pltpu.with_memory_space_constraint(array, pltpu.VMEM)


def hold_kernel(given_ref, held_ref, sems):
    rows = given_ref.shape[0] // HOLDS
    copies = []
    for k in range(HOLDS):
        part = pl.ds(k * rows, rows)
        copy = pltpu.make_async_copy(given_ref.at[part], held_ref.at[part], sems.at[k])
        copy.start()
        copies.append(copy)
    for copy in copies:
        copy.wait()


def hold(given):
    given = pltpu.with_memory_space_constraint(given, pltpu.HBM)
    return pl.pallas_call(
        hold_kernel,
        out_shape=pltpu.VMEM(given.shape, given.dtype),
        in_specs=[pl.BlockSpec(memory_space=pl.ANY)],
        out_specs=VMEM,
        scratch_shapes=[pltpu.SemaphoreType.DMA((HOLDS,))],
        compiler_params=PARAMS,
        cost_estimate=pl.CostEstimate(
            flops=0, bytes_accessed=4 * given.size, transcendentals=0
        ),
        name="hold",
    )(given)


def load_kernel(
    place_ref, test_ref, grads_ref, kept_ref, sent_ref, held_ref, test_held, sems, test_sems
):
    width = grads_ref.shape[1] // CHUNKS
    copies = []
    for k in range(CHUNKS):
        cols = pl.ds(k * width, width)
        first = pltpu.make_async_copy(
            test_ref.at[:, cols], test_held.at[:, cols], test_sems.at[k]
        )
        second = pltpu.make_async_copy(
            grads_ref.at[:, cols], held_ref.at[:, cols], sems.at[k]
        )
        first.start()
        second.start()
        copies.append((first, second))
    total = None
    for k in range(CHUNKS):
        cols = pl.ds(k * width, width)
        copies[k][0].wait()
        copies[k][1].wait()
        step = dot(test_held[:, cols], held_ref[:, cols], ((1,), (1,)))
        total = step if total is None else total + step
    first = place_ref[1] == 0
    kept_ref[...] = jnp.where(first, total[:HALF], total[HALF:]).astype(BF16)
    sent_ref[...] = jnp.where(first, total[HALF:], total[:HALF]).astype(BF16)


def load_and_sketch(place, test_t, grads):
    rows, cols = grads.shape
    test_t = pltpu.with_memory_space_constraint(test_t, pltpu.HBM)
    grads = pltpu.with_memory_space_constraint(grads, pltpu.HBM)
    part = jax.ShapeDtypeStruct((HALF, rows), BF16)
    return pl.pallas_call(
        load_kernel,
        out_shape=(part, part, pltpu.VMEM((rows, cols), BF16)),
        in_specs=[SMEM] + [pl.BlockSpec(memory_space=pl.ANY)] * 2,
        out_specs=(VMEM,) * 3,
        scratch_shapes=[
            pltpu.VMEM((K, cols), BF16),
            pltpu.SemaphoreType.DMA((CHUNKS,)),
            pltpu.SemaphoreType.DMA((CHUNKS,)),
        ],
        compiler_params=PARAMS,
        cost_estimate=cost(grads),
        name="load_and_sketch",
    )(place, test_t, grads)


def summed_small(place_ref, refs, scale):
    total = refs[0][...].astype(F32)
    for ref in refs[1:]:
        total = total + ref[...].astype(F32)
    rows = total.shape[1] // 2
    slot = lax.broadcasted_iota(jnp.int32, total.shape, 1)
    own = slot < place_ref[2]
    other = (slot >= rows) & (slot < place_ref[3] + rows)
    return jnp.where(own | other, total * scale, 0.0).astype(BF16)


def token_kernel(scale, place_ref, *refs):
    own_ref, other_ref, part_ref = refs[-3:]
    small = summed_small(place_ref, refs[:-3], scale)
    rows = own_ref.shape[0]
    for k in range(own_ref.shape[1] // BLOCK):
        cols = slice(k * BLOCK, (k + 1) * BLOCK)
        out = dot(small[:, :rows], own_ref[:, cols], ((1,), (0,)))
        out = out + dot(small[:, rows:], other_ref[:, cols], ((1,), (0,)))
        part_ref[:, cols] = out.astype(BF16)


def token_part(place, pieces, own, other, scale):
    return pl.pallas_call(
        functools.partial(token_kernel, scale),
        out_shape=jax.ShapeDtypeStruct((HALF, own.shape[1]), BF16),
        in_specs=[SMEM] + [VMEM] * (len(pieces) + 2),
        out_specs=VMEM,
        compiler_params=PARAMS,
        cost_estimate=cost(own),
        name="token_part",
    )(place, *pieces, in_vmem(own), in_vmem(other))


def feature_kernel(small_ref, own_ref, other_ref, part_ref):
    rows = own_ref.shape[0]
    for at, big_ref in ((0, own_ref), (rows, other_ref)):
        total = None
        for k in range(big_ref.shape[1] // BLOCK):
            cols = slice(k * BLOCK, (k + 1) * BLOCK)
            step = dot(small_ref[:, cols], big_ref[:, cols], ((1,), (1,)))
            total = step if total is None else total + step
        part_ref[:, at : at + rows] = total.astype(BF16)


def feature_part(small, own, other):
    return pl.pallas_call(
        feature_kernel,
        out_shape=jax.ShapeDtypeStruct((HALF, 2 * own.shape[0]), BF16),
        in_specs=[VMEM] * 3,
        out_specs=VMEM,
        compiler_params=PARAMS,
        cost_estimate=cost(own),
        name="feature_part",
    )(small, in_vmem(own), in_vmem(other))


def up_kernel(place_ref, *refs):
    own_ref, other_ref, part_ref, gram_ref = refs[-4:]
    rows = own_ref.shape[0]
    pieces = [ref.at[:, : 2 * rows] for ref in refs[:-4]]
    small = summed_small(place_ref, pieces, 1.0)
    gram = None
    for ref in refs[:-4]:
        high = ref[:, 2 * rows : 2 * rows + 128].astype(F32)
        low = ref[:, 2 * rows + 128 : 2 * rows + 256].astype(F32)
        gram = high + low if gram is None else gram + (high + low)
    gram_ref[...] = gram
    width = own_ref.shape[1] // 32
    lane = lax.broadcasted_iota(jnp.int32, (HALF, 256), 1)
    high = (place_ref[2] // 32 + place_ref[3] // 32).astype(F32)
    low = (place_ref[2] % 32 + place_ref[3] % 32).astype(F32)
    digits = jnp.where(lane == width, high, jnp.where(lane == width + 1, low, 0.0))
    tail = digits.astype(BF16)[:, width:]
    for z in range(8):
        cols = slice(4 * z * width, 4 * (z + 1) * width)
        out = dot(small[:, :rows], own_ref[:, cols], ((1,), (0,)))
        out = out + dot(small[:, rows:], other_ref[:, cols], ((1,), (0,)))
        out = out.astype(BF16)
        for x in range(4):
            piece = out[:, x * width : (x + 1) * width]
            part_ref[8 * x + z] = jnp.concatenate([piece, tail], 1)


def up_part(place, pieces, own, other):
    return pl.pallas_call(
        up_kernel,
        out_shape=(
            jax.ShapeDtypeStruct((32, HALF, 256), BF16),
            jax.ShapeDtypeStruct((HALF, 128), F32),
        ),
        in_specs=[SMEM] + [VMEM] * (len(pieces) + 2),
        out_specs=(VMEM, VMEM),
        compiler_params=PARAMS,
        cost_estimate=cost(own),
        name="up_part",
    )(place, *pieces, in_vmem(own), in_vmem(other))


def split_kernel(place_ref, pieces_ref, kept_ref, sent_ref):
    owned = kept_ref.shape[1] - 16
    total = pieces_ref[0].astype(F32)
    for k in range(1, pieces_ref.shape[0]):
        total = total + pieces_ref[k].astype(F32)
    tail = total[:, 2 * owned : 2 * owned + 16]
    first = jnp.concatenate([total[:, :owned], tail], 1)
    second = total[:, owned : 2 * owned + 16]
    mine = place_ref[1] == 0
    kept_ref[...] = jnp.where(mine, first, second)
    sent_ref[...] = jnp.where(mine, second, first)


def split_up(place, pieces, owned):
    shape = jax.ShapeDtypeStruct((HALF, owned + 16), F32)
    return pl.pallas_call(
        split_kernel,
        out_shape=(shape, shape),
        in_specs=[SMEM, VMEM],
        out_specs=(VMEM, VMEM),
        compiler_params=PARAMS,
        name="split_up",
    )(place, pieces)


def finish_kernel(place_ref, kept_ref, came_ref, inverse_ref, up_ref):
    owned = up_ref.shape[1]
    kept, came = kept_ref[...], came_ref[...]
    high, low = kept[:1, owned : owned + 1], kept[:1, owned + 1 : owned + 2]
    inv_root = lax.rsqrt(32.0 * high + low)
    mine = place_ref[1] == 0
    total = jnp.concatenate([jnp.where(mine, kept, came), jnp.where(mine, came, kept)], 0)
    up = lax.dot_general(
        inverse_ref[...],
        total,
        (((1,), (0,)), ((), ())),
        precision=lax.Precision.HIGHEST,
        preferred_element_type=F32,
    )
    up_ref[...] = (inv_root * up)[:, :owned]


def finish_up(place, kept, came, inverse, owned):
    return pl.pallas_call(
        finish_kernel,
        out_shape=jax.ShapeDtypeStruct((K, owned), F32),
        in_specs=[SMEM] + [VMEM] * 3,
        out_specs=VMEM,
        compiler_params=PARAMS,
        name="finish_up",
    )(place, kept, came, inverse)


def both_halves(first, own, other):
    return jnp.where(
        first, jnp.concatenate([own, other], 0), jnp.concatenate([other, own], 0)
    )


def aligned(block):
    return jnp.pad(block, ((0, 0), (0, 128 - block.shape[1])))


def local(tokens, out_grads, test_matrix, slot_counts):
    spots = jnp.stack([lax.axis_index(("z", "x", "c")), lax.axis_index("c")])
    place = jnp.concatenate([spots, slot_counts, sibling(slot_counts)])
    scale = LIVE ** -0.5
    width = tokens.shape[1] // 64

    kept, sent, grads = load_and_sketch(spots, test_matrix.T, out_grads)
    sketch_part = jnp.concatenate([kept, sibling(sent)], 1)
    other_tokens, sketch_part = lax.optimization_barrier((sibling(tokens), sketch_part))
    sent_grads, sketch_part = lax.optimization_barrier((out_grads, sketch_part))
    other_grads = sibling(sent_grads)
    other_tokens = hold(other_tokens)

    ranged = chips_sum(
        token_part(place, y_pieces(sketch_part), tokens, other_tokens, 1.0), scale
    )
    back_part = feature_part(ranged, tokens, other_tokens)
    other_grads, back_part = lax.optimization_barrier((other_grads, back_part))
    back = y_pieces(back_part)
    other_grads = hold(other_grads)
    transposed = chips_sum(
        token_part(place, back, grads, other_grads, D ** -0.5), scale, ("x", "z")
    )
    again = y_pieces(feature_part(transposed, grads, other_grads))
    whole_range = chips_sum(
        token_part(place, again, tokens, other_tokens, FF ** -0.5), scale
    )

    other_range = sibling(whole_range)
    both = jnp.concatenate([whole_range, other_range], 0)
    gram_part = dot(whole_range, both, ((1,), (1,)))
    high = gram_part.astype(BF16)
    low = (gram_part - high.astype(F32)).astype(BF16)
    projected = feature_part(whole_range, tokens, other_tokens)
    joined = y_pieces(jnp.concatenate([projected, aligned(high), aligned(low)], 1))

    up, gram_rows = up_part(place, joined, grads, other_grads)
    up_pieces = exchange(up, ("x", "z"))
    gram_rows, place = lax.optimization_barrier((gram_rows, place))
    gram_rows = gram_rows[:, :K]
    first = place[1] == 0
    other_rows = sibling(gram_rows)
    other_rows = jnp.roll(other_rows, HALF, 1)
    gram = both_halves(first, gram_rows, other_rows)
    gram = jnp.where(first, gram, jnp.roll(gram, HALF, 1))
    lower = jnp.linalg.cholesky(gram)
    inverse = lax.linalg.triangular_solve(
        lower, jnp.eye(K, dtype=F32), left_side=True, lower=True
    )

    owned = out_grads.shape[1] // 64
    kept_up, sent_up = split_up(place, up_pieces, owned)
    adapter_up = finish_up(place, kept_up, sibling(sent_up), inverse, owned).T

    own = both_halves(first, whole_range, other_range)
    own = lax.dynamic_slice_in_dim(own, place[0] * width, width, 1).astype(F32)
    adapter_down = jnp.dot(inverse, own, precision=lax.Precision.HIGHEST).T * D ** 0.5
    return adapter_down, adapter_up


def solution(mesh):
    split = Mesh(mesh.devices.reshape(8, 4, 2, 4), ("z", "x", "c", "y"))
    dp = ("z", "x", "c")
    placed = (P(dp, "y"), P(dp, "y"), P("y", None), P(dp))
    return jax.shard_map(
        local,
        mesh=split,
        in_specs=placed,
        out_specs=(P(("y",) + dp, None), P(("y",) + dp, None)),
        check_vma=False,
    )
```

```python
import functools

import jax
import jax.numpy as jnp
from jax import lax
from jax.experimental import pallas as pl
from jax.experimental.pallas import tpu as pltpu
from jax.sharding import Mesh, PartitionSpec as P

D = 8192
FF = 28672
K = 80
HALF = K // 2
LIVE = 16384
F32 = jnp.float32
BF16 = jnp.bfloat16
CHUNKS = 14
BLOCK = 1024
HOLDS = 8
VMEM = pl.BlockSpec(memory_space=pltpu.VMEM)
SMEM = pl.BlockSpec(memory_space=pltpu.SMEM)
PARAMS = pltpu.CompilerParams(vmem_limit_bytes=16 << 20)


def dot(left, right, contract):
    return lax.dot_general(left, right, (contract, ((), ())), preferred_element_type=F32)


def shifted(value, axis, size, step):
    return lax.ppermute(value, axis, [(i, (i + step) % size) for i in range(size)])


def sibling(value):
    return shifted(value, "c", 2, 1)


def y_pieces(sent):
    return [sent] + [shifted(sent, "y", 4, step) for step in (3, 2, 1)]


def to_tiles(array):
    rows, cols = array.shape
    tiles = array.reshape(rows // 8, 8, cols // 128, 128).transpose(0, 2, 1, 3)
    return tiles.reshape(-1, 8, 128)


def from_tiles(tiles, rows, cols):
    split = tiles.reshape(rows // 8, cols // 128, 8, 128).transpose(0, 2, 1, 3)
    return split.reshape(rows, cols)


def exchange(pieces, axes):
    return lax.all_to_all(pieces, axes, 0, 0, tiled=True)


def spread(piece, axes, count):
    return exchange(jnp.broadcast_to(piece[None], (count,) + piece.shape), axes)


def chips_sum(part, scale, axes=("z", "x")):
    rows, cols = part.shape
    tiles = to_tiles(part)
    count = tiles.shape[0]
    per = -(-count // 32)
    tiles = jnp.pad(tiles, ((0, 32 * per - count), (0, 0), (0, 0)))
    pieces = tiles.reshape(32, per, 8, 128)
    mine = (exchange(pieces, axes).astype(F32).sum(0) * scale).astype(BF16)
    whole = spread(mine, axes, 32).reshape(32 * per, 8, 128)[:count]
    return from_tiles(whole, rows, cols)


def cost(big):
    rows, cols = big.shape
    return pl.CostEstimate(
        flops=4 * HALF * rows * cols, bytes_accessed=4 * rows * cols, transcendentals=0
    )


def in_vmem(array):
    return pltpu.with_memory_space_constraint(array, pltpu.VMEM)


def hold_kernel(given_ref, held_ref, sems):
    rows = given_ref.shape[0] // HOLDS
    copies = []
    for k in range(HOLDS):
        part = pl.ds(k * rows, rows)
        copy = pltpu.make_async_copy(given_ref.at[part], held_ref.at[part], sems.at[k])
        copy.start()
        copies.append(copy)
    for copy in copies:
        copy.wait()


def hold(given):
    given = pltpu.with_memory_space_constraint(given, pltpu.HBM)
    return pl.pallas_call(
        hold_kernel,
        out_shape=pltpu.VMEM(given.shape, given.dtype),
        in_specs=[pl.BlockSpec(memory_space=pl.ANY)],
        out_specs=VMEM,
        scratch_shapes=[pltpu.SemaphoreType.DMA((HOLDS,))],
        compiler_params=PARAMS,
        cost_estimate=pl.CostEstimate(
            flops=0, bytes_accessed=4 * given.size, transcendentals=0
        ),
        name="hold",
    )(given)


def load_kernel(
    place_ref, test_ref, grads_ref, kept_ref, sent_ref, held_ref, test_held, sems, test_sems
):
    width = grads_ref.shape[1] // CHUNKS
    copies = []
    for k in range(CHUNKS):
        cols = pl.ds(k * width, width)
        first = pltpu.make_async_copy(
            test_ref.at[:, cols], test_held.at[:, cols], test_sems.at[k]
        )
        second = pltpu.make_async_copy(
            grads_ref.at[:, cols], held_ref.at[:, cols], sems.at[k]
        )
        first.start()
        second.start()
        copies.append((first, second))
    total = None
    for k in range(CHUNKS):
        cols = pl.ds(k * width, width)
        copies[k][0].wait()
        copies[k][1].wait()
        step = dot(test_held[:, cols], held_ref[:, cols], ((1,), (1,)))
        total = step if total is None else total + step
    first = place_ref[1] == 0
    kept_ref[...] = jnp.where(first, total[:HALF], total[HALF:]).astype(BF16)
    sent_ref[...] = jnp.where(first, total[HALF:], total[:HALF]).astype(BF16)


def load_and_sketch(place, test_t, grads):
    rows, cols = grads.shape
    test_t = pltpu.with_memory_space_constraint(test_t, pltpu.HBM)
    grads = pltpu.with_memory_space_constraint(grads, pltpu.HBM)
    part = jax.ShapeDtypeStruct((HALF, rows), BF16)
    return pl.pallas_call(
        load_kernel,
        out_shape=(part, part, pltpu.VMEM((rows, cols), BF16)),
        in_specs=[SMEM] + [pl.BlockSpec(memory_space=pl.ANY)] * 2,
        out_specs=(VMEM,) * 3,
        scratch_shapes=[
            pltpu.VMEM((K, cols), BF16),
            pltpu.SemaphoreType.DMA((CHUNKS,)),
            pltpu.SemaphoreType.DMA((CHUNKS,)),
        ],
        compiler_params=PARAMS,
        cost_estimate=cost(grads),
        name="load_and_sketch",
    )(place, test_t, grads)


def summed_small(place_ref, refs, scale):
    total = refs[0][...].astype(F32)
    for ref in refs[1:]:
        total = total + ref[...].astype(F32)
    rows = total.shape[1] // 2
    slot = lax.broadcasted_iota(jnp.int32, total.shape, 1)
    own = slot < place_ref[2]
    other = (slot >= rows) & (slot < place_ref[3] + rows)
    return jnp.where(own | other, total * scale, 0.0).astype(BF16)


def token_kernel(scale, place_ref, *refs):
    own_ref, other_ref, part_ref = refs[-3:]
    small = summed_small(place_ref, refs[:-3], scale)
    rows = own_ref.shape[0]
    for k in range(own_ref.shape[1] // BLOCK):
        cols = slice(k * BLOCK, (k + 1) * BLOCK)
        out = dot(small[:, :rows], own_ref[:, cols], ((1,), (0,)))
        out = out + dot(small[:, rows:], other_ref[:, cols], ((1,), (0,)))
        part_ref[:, cols] = out.astype(BF16)


def token_part(place, pieces, own, other, scale):
    return pl.pallas_call(
        functools.partial(token_kernel, scale),
        out_shape=jax.ShapeDtypeStruct((HALF, own.shape[1]), BF16),
        in_specs=[SMEM] + [VMEM] * (len(pieces) + 2),
        out_specs=VMEM,
        compiler_params=PARAMS,
        cost_estimate=cost(own),
        name="token_part",
    )(place, *pieces, in_vmem(own), in_vmem(other))


def feature_kernel(small_ref, own_ref, other_ref, part_ref):
    rows = own_ref.shape[0]
    for at, big_ref in ((0, own_ref), (rows, other_ref)):
        total = None
        for k in range(big_ref.shape[1] // BLOCK):
            cols = slice(k * BLOCK, (k + 1) * BLOCK)
            step = dot(small_ref[:, cols], big_ref[:, cols], ((1,), (1,)))
            total = step if total is None else total + step
        part_ref[:, at : at + rows] = total.astype(BF16)


def feature_part(small, own, other):
    return pl.pallas_call(
        feature_kernel,
        out_shape=jax.ShapeDtypeStruct((HALF, 2 * own.shape[0]), BF16),
        in_specs=[VMEM] * 3,
        out_specs=VMEM,
        compiler_params=PARAMS,
        cost_estimate=cost(own),
        name="feature_part",
    )(small, in_vmem(own), in_vmem(other))


def up_kernel(place_ref, *refs):
    own_ref, other_ref, part_ref, gram_ref = refs[-4:]
    rows = own_ref.shape[0]
    pieces = [ref.at[:, : 2 * rows] for ref in refs[:-4]]
    small = summed_small(place_ref, pieces, 1.0)
    gram = None
    for ref in refs[:-4]:
        high = ref[:, 2 * rows : 2 * rows + 128].astype(F32)
        low = ref[:, 2 * rows + 128 : 2 * rows + 256].astype(F32)
        gram = high + low if gram is None else gram + (high + low)
    gram_ref[...] = gram
    width = own_ref.shape[1] // 32
    lane = lax.broadcasted_iota(jnp.int32, (HALF, 256), 1)
    high = (place_ref[2] // 32 + place_ref[3] // 32).astype(F32)
    low = (place_ref[2] % 32 + place_ref[3] % 32).astype(F32)
    digits = jnp.where(lane == width, high, jnp.where(lane == width + 1, low, 0.0))
    tail = digits.astype(BF16)[:, width:]
    for z in range(8):
        cols = slice(4 * z * width, 4 * (z + 1) * width)
        out = dot(small[:, :rows], own_ref[:, cols], ((1,), (0,)))
        out = out + dot(small[:, rows:], other_ref[:, cols], ((1,), (0,)))
        out = out.astype(BF16)
        for x in range(4):
            piece = out[:, x * width : (x + 1) * width]
            part_ref[8 * x + z] = jnp.concatenate([piece, tail], 1)


def up_part(place, pieces, own, other):
    return pl.pallas_call(
        up_kernel,
        out_shape=(
            jax.ShapeDtypeStruct((32, HALF, 256), BF16),
            jax.ShapeDtypeStruct((HALF, 128), F32),
        ),
        in_specs=[SMEM] + [VMEM] * (len(pieces) + 2),
        out_specs=(VMEM, VMEM),
        compiler_params=PARAMS,
        cost_estimate=cost(own),
        name="up_part",
    )(place, *pieces, in_vmem(own), in_vmem(other))


def split_kernel(place_ref, pieces_ref, kept_ref, sent_ref):
    owned = kept_ref.shape[1] - 16
    total = pieces_ref[0].astype(F32)
    for k in range(1, pieces_ref.shape[0]):
        total = total + pieces_ref[k].astype(F32)
    tail = total[:, 2 * owned : 2 * owned + 16]
    first = jnp.concatenate([total[:, :owned], tail], 1)
    second = total[:, owned : 2 * owned + 16]
    mine = place_ref[1] == 0
    kept_ref[...] = jnp.where(mine, first, second)
    sent_ref[...] = jnp.where(mine, second, first)


def split_up(place, pieces, owned):
    shape = jax.ShapeDtypeStruct((HALF, owned + 16), F32)
    return pl.pallas_call(
        split_kernel,
        out_shape=(shape, shape),
        in_specs=[SMEM, VMEM],
        out_specs=(VMEM, VMEM),
        compiler_params=PARAMS,
        name="split_up",
    )(place, pieces)


def finish_kernel(place_ref, kept_ref, came_ref, inverse_ref, up_ref):
    owned = up_ref.shape[1]
    kept, came = kept_ref[...], came_ref[...]
    high, low = kept[:1, owned : owned + 1], kept[:1, owned + 1 : owned + 2]
    inv_root = lax.rsqrt(32.0 * high + low)
    mine = place_ref[1] == 0
    total = jnp.concatenate([jnp.where(mine, kept, came), jnp.where(mine, came, kept)], 0)
    up = lax.dot_general(
        inverse_ref[...],
        total,
        (((1,), (0,)), ((), ())),
        precision=lax.Precision.HIGHEST,
        preferred_element_type=F32,
    )
    up_ref[...] = (inv_root * up)[:, :owned]


def finish_up(place, kept, came, inverse, owned):
    return pl.pallas_call(
        finish_kernel,
        out_shape=jax.ShapeDtypeStruct((K, owned), F32),
        in_specs=[SMEM] + [VMEM] * 3,
        out_specs=VMEM,
        compiler_params=PARAMS,
        name="finish_up",
    )(place, kept, came, inverse)


def both_halves(first, own, other):
    return jnp.where(
        first, jnp.concatenate([own, other], 0), jnp.concatenate([other, own], 0)
    )


def aligned(block):
    return jnp.pad(block, ((0, 0), (0, 128 - block.shape[1])))


def local(tokens, out_grads, test_matrix, slot_counts):
    spots = jnp.stack([lax.axis_index(("z", "x", "c")), lax.axis_index("c")])
    place = jnp.concatenate([spots, slot_counts, sibling(slot_counts)])
    scale = LIVE ** -0.5
    width = tokens.shape[1] // 64

    kept, sent, grads = load_and_sketch(spots, test_matrix.T, out_grads)
    sketch_part = jnp.concatenate([kept, sibling(sent)], 1)
    other_tokens, sketch_part = lax.optimization_barrier((sibling(tokens), sketch_part))
    sent_grads, sketch_part = lax.optimization_barrier((out_grads, sketch_part))
    other_grads = sibling(sent_grads)
    other_tokens = hold(other_tokens)

    ranged = chips_sum(
        token_part(place, y_pieces(sketch_part), tokens, other_tokens, 1.0), scale
    )
    back_part = feature_part(ranged, tokens, other_tokens)
    other_grads, back_part = lax.optimization_barrier((other_grads, back_part))
    back = y_pieces(back_part)
    other_grads = hold(other_grads)
    transposed = chips_sum(
        token_part(place, back, grads, other_grads, D ** -0.5), scale, ("x", "z")
    )
    again = y_pieces(feature_part(transposed, grads, other_grads))
    whole_range = chips_sum(
        token_part(place, again, tokens, other_tokens, FF ** -0.5), scale
    )

    other_range = sibling(whole_range)
    both = jnp.concatenate([whole_range, other_range], 0)
    gram_part = dot(both, both, ((1,), (1,)))
    gram_part = jnp.concatenate([gram_part[:HALF], gram_part[HALF:, HALF:]], 1)
    high = gram_part.astype(BF16)
    low = (gram_part - high.astype(F32)).astype(BF16)
    projected = feature_part(whole_range, tokens, other_tokens)
    joined = y_pieces(jnp.concatenate([projected, aligned(high), aligned(low)], 1))

    up, gram_rows = up_part(place, joined, grads, other_grads)
    up_pieces = exchange(up, ("x", "z"))
    gram_rows, place = lax.optimization_barrier((gram_rows, place))
    own_rows, corner = gram_rows[:, :K], gram_rows[:, K : K + HALF]
    other_rows = jnp.concatenate([own_rows[:, HALF:].T, corner], 1)
    gram = jnp.concatenate([own_rows, other_rows], 0)
    first = place[1] == 0
    gram = jnp.where(first, gram, jnp.roll(gram, (HALF, HALF), (0, 1)))
    lower = jnp.linalg.cholesky(gram)
    inverse = lax.linalg.triangular_solve(
        lower, jnp.eye(K, dtype=F32), left_side=True, lower=True
    )

    owned = out_grads.shape[1] // 64
    kept_up, sent_up = split_up(place, up_pieces, owned)
    adapter_up = finish_up(place, kept_up, sibling(sent_up), inverse, owned).T

    own = both_halves(first, whole_range, other_range)
    own = lax.dynamic_slice_in_dim(own, place[0] * width, width, 1).astype(F32)
    adapter_down = jnp.dot(inverse, own, precision=lax.Precision.HIGHEST).T * D ** 0.5
    return adapter_down, adapter_up


def solution(mesh):
    split = Mesh(mesh.devices.reshape(8, 4, 2, 4), ("z", "x", "c", "y"))
    dp = ("z", "x", "c")
    placed = (P(dp, "y"), P(dp, "y"), P("y", None), P(dp))
    return jax.shard_map(
        local,
        mesh=split,
        in_specs=placed,
        out_specs=(P(("y",) + dp, None), P(("y",) + dp, None)),
        check_vma=False,
    )
```

```python
import functools

import jax
import jax.numpy as jnp
from jax import lax
from jax.experimental import pallas as pl
from jax.experimental.pallas import tpu as pltpu
from jax.sharding import Mesh, PartitionSpec as P

D = 8192
FF = 28672
K = 80
HALF = K // 2
LIVE = 16384
F32 = jnp.float32
BF16 = jnp.bfloat16
CHUNKS = 14
BLOCK = 1024
HOLDS = 8
VMEM = pl.BlockSpec(memory_space=pltpu.VMEM)
SMEM = pl.BlockSpec(memory_space=pltpu.SMEM)
PARAMS = pltpu.CompilerParams(vmem_limit_bytes=16 << 20)


def dot(left, right, contract):
    return lax.dot_general(left, right, (contract, ((), ())), preferred_element_type=F32)


def shifted(value, axis, size, step):
    return lax.ppermute(value, axis, [(i, (i + step) % size) for i in range(size)])


def sibling(value):
    return shifted(value, "c", 2, 1)


def y_pieces(sent):
    return [sent] + [shifted(sent, "y", 4, step) for step in (3, 2, 1)]


def to_tiles(array):
    rows, cols = array.shape
    tiles = array.reshape(rows // 8, 8, cols // 128, 128).transpose(0, 2, 1, 3)
    return tiles.reshape(-1, 8, 128)


def from_tiles(tiles, rows, cols):
    split = tiles.reshape(rows // 8, cols // 128, 8, 128).transpose(0, 2, 1, 3)
    return split.reshape(rows, cols)


def exchange(pieces, axes):
    return lax.all_to_all(pieces, axes, 0, 0, tiled=True)


def spread(piece, axes, count):
    return exchange(jnp.broadcast_to(piece[None], (count,) + piece.shape), axes)


def chips_sum(part, scale, axes=("z", "x")):
    rows, cols = part.shape
    tiles = to_tiles(part)
    count = tiles.shape[0]
    per = -(-count // 32)
    tiles = jnp.pad(tiles, ((0, 32 * per - count), (0, 0), (0, 0)))
    pieces = tiles.reshape(32, per, 8, 128)
    mine = (exchange(pieces, axes).astype(F32).sum(0) * scale).astype(BF16)
    whole = spread(mine, axes, 32).reshape(32 * per, 8, 128)[:count]
    return from_tiles(whole, rows, cols)


def cost(big):
    rows, cols = big.shape
    return pl.CostEstimate(
        flops=4 * HALF * rows * cols, bytes_accessed=4 * rows * cols, transcendentals=0
    )


def in_vmem(array):
    return pltpu.with_memory_space_constraint(array, pltpu.VMEM)


def hold_kernel(given_ref, held_ref, sems):
    rows = given_ref.shape[0] // HOLDS
    copies = []
    for k in range(HOLDS):
        part = pl.ds(k * rows, rows)
        copy = pltpu.make_async_copy(given_ref.at[part], held_ref.at[part], sems.at[k])
        copy.start()
        copies.append(copy)
    for copy in copies:
        copy.wait()


def hold(given):
    given = pltpu.with_memory_space_constraint(given, pltpu.HBM)
    return pl.pallas_call(
        hold_kernel,
        out_shape=pltpu.VMEM(given.shape, given.dtype),
        in_specs=[pl.BlockSpec(memory_space=pl.ANY)],
        out_specs=VMEM,
        scratch_shapes=[pltpu.SemaphoreType.DMA((HOLDS,))],
        compiler_params=PARAMS,
        cost_estimate=pl.CostEstimate(
            flops=0, bytes_accessed=4 * given.size, transcendentals=0
        ),
        name="hold",
    )(given)


def load_kernel(
    place_ref, test_ref, grads_ref, kept_ref, sent_ref, held_ref, test_held, sems, test_sems
):
    width = grads_ref.shape[1] // CHUNKS
    copies = []
    for k in range(CHUNKS):
        cols = pl.ds(k * width, width)
        first = pltpu.make_async_copy(
            test_ref.at[:, cols], test_held.at[:, cols], test_sems.at[k]
        )
        second = pltpu.make_async_copy(
            grads_ref.at[:, cols], held_ref.at[:, cols], sems.at[k]
        )
        first.start()
        second.start()
        copies.append((first, second))
    total = None
    for k in range(CHUNKS):
        cols = pl.ds(k * width, width)
        copies[k][0].wait()
        copies[k][1].wait()
        step = dot(test_held[:, cols], held_ref[:, cols], ((1,), (1,)))
        total = step if total is None else total + step
    first = place_ref[1] == 0
    kept_ref[...] = jnp.where(first, total[:HALF], total[HALF:]).astype(BF16)
    sent_ref[...] = jnp.where(first, total[HALF:], total[:HALF]).astype(BF16)


def load_and_sketch(place, test_t, grads):
    rows, cols = grads.shape
    test_t = pltpu.with_memory_space_constraint(test_t, pltpu.HBM)
    grads = pltpu.with_memory_space_constraint(grads, pltpu.HBM)
    part = jax.ShapeDtypeStruct((HALF, rows), BF16)
    return pl.pallas_call(
        load_kernel,
        out_shape=(part, part, pltpu.VMEM((rows, cols), BF16)),
        in_specs=[SMEM] + [pl.BlockSpec(memory_space=pl.ANY)] * 2,
        out_specs=(VMEM,) * 3,
        scratch_shapes=[
            pltpu.VMEM((K, cols), BF16),
            pltpu.SemaphoreType.DMA((CHUNKS,)),
            pltpu.SemaphoreType.DMA((CHUNKS,)),
        ],
        compiler_params=PARAMS,
        cost_estimate=cost(grads),
        name="load_and_sketch",
    )(place, test_t, grads)


def summed_small(place_ref, refs, scale):
    total = refs[0][...].astype(F32)
    for ref in refs[1:]:
        total = total + ref[...].astype(F32)
    rows = total.shape[1] // 2
    slot = lax.broadcasted_iota(jnp.int32, total.shape, 1)
    own = slot < place_ref[2]
    other = (slot >= rows) & (slot < place_ref[3] + rows)
    return jnp.where(own | other, total * scale, 0.0).astype(BF16)


def token_kernel(scale, place_ref, *refs):
    own_ref, other_ref, part_ref = refs[-3:]
    small = summed_small(place_ref, refs[:-3], scale)
    rows = own_ref.shape[0]
    for k in range(own_ref.shape[1] // BLOCK):
        cols = slice(k * BLOCK, (k + 1) * BLOCK)
        out = dot(small[:, :rows], own_ref[:, cols], ((1,), (0,)))
        out = out + dot(small[:, rows:], other_ref[:, cols], ((1,), (0,)))
        part_ref[:, cols] = out.astype(BF16)


def token_part(place, pieces, own, other, scale):
    return pl.pallas_call(
        functools.partial(token_kernel, scale),
        out_shape=jax.ShapeDtypeStruct((HALF, own.shape[1]), BF16),
        in_specs=[SMEM] + [VMEM] * (len(pieces) + 2),
        out_specs=VMEM,
        compiler_params=PARAMS,
        cost_estimate=cost(own),
        name="token_part",
    )(place, *pieces, in_vmem(own), in_vmem(other))


def feature_kernel(small_ref, own_ref, other_ref, part_ref):
    rows = own_ref.shape[0]
    for at, big_ref in ((0, own_ref), (rows, other_ref)):
        total = None
        for k in range(big_ref.shape[1] // BLOCK):
            cols = slice(k * BLOCK, (k + 1) * BLOCK)
            step = dot(small_ref[:, cols], big_ref[:, cols], ((1,), (1,)))
            total = step if total is None else total + step
        part_ref[:, at : at + rows] = total.astype(BF16)


def feature_part(small, own, other):
    return pl.pallas_call(
        feature_kernel,
        out_shape=jax.ShapeDtypeStruct((HALF, 2 * own.shape[0]), BF16),
        in_specs=[VMEM] * 3,
        out_specs=VMEM,
        compiler_params=PARAMS,
        cost_estimate=cost(own),
        name="feature_part",
    )(small, in_vmem(own), in_vmem(other))


def up_kernel(place_ref, *refs):
    own_ref, other_ref, part_ref, gram_ref = refs[-4:]
    rows = own_ref.shape[0]
    pieces = [ref.at[:, : 2 * rows] for ref in refs[:-4]]
    small = summed_small(place_ref, pieces, 1.0)
    gram = None
    for ref in refs[:-4]:
        high = ref[:, 2 * rows : 2 * rows + 128].astype(F32)
        low = ref[:, 2 * rows + 128 : 2 * rows + 256].astype(F32)
        gram = high + low if gram is None else gram + (high + low)
    gram_ref[...] = gram
    width = own_ref.shape[1] // 32
    over = width - 128
    lane = lax.broadcasted_iota(jnp.int32, (8, 128 - over), 1)
    high = (place_ref[2] // 32 + place_ref[3] // 32).astype(F32)
    low = (place_ref[2] % 32 + place_ref[3] % 32).astype(F32)
    digits = jnp.where(lane == 0, high, jnp.where(lane == 1, low, 0.0))
    for z in range(8):
        cols = slice(4 * z * width, 4 * (z + 1) * width)
        out = dot(small[:, :rows], own_ref[:, cols], ((1,), (0,)))
        out = out + dot(small[:, rows:], other_ref[:, cols], ((1,), (0,)))
        for x in range(4):
            piece = out[:, x * width : (x + 1) * width]
            rest = piece[:, 128:]
            last = rest[32:]
            beside = [last[:, 32 * i : 32 * i + 32] for i in range(3)] + [digits]
            for i in range(5):
                part_ref[8 * x + z, i] = piece[8 * i : 8 * i + 8, :128].astype(BF16)
            for i in range(4):
                tile = jnp.concatenate([rest[8 * i : 8 * i + 8], beside[i]], 1)
                part_ref[8 * x + z, 5 + i] = tile.astype(BF16)


def up_part(place, pieces, own, other):
    return pl.pallas_call(
        up_kernel,
        out_shape=(
            jax.ShapeDtypeStruct((32, 9, 8, 128), BF16),
            jax.ShapeDtypeStruct((HALF, 128), F32),
        ),
        in_specs=[SMEM] + [VMEM] * (len(pieces) + 2),
        out_specs=(VMEM, VMEM),
        compiler_params=PARAMS,
        cost_estimate=cost(own),
        name="up_part",
    )(place, *pieces, in_vmem(own), in_vmem(other))


def split_kernel(place_ref, pieces_ref, kept_ref, sent_ref):
    owned = kept_ref.shape[1] - 16
    total = pieces_ref[0].astype(F32)
    for k in range(1, pieces_ref.shape[0]):
        total = total + pieces_ref[k].astype(F32)
    over = 2 * owned - 128
    last = jnp.concatenate([total[5 + i][:, over:] for i in range(3)], 1)
    wide = jnp.concatenate([total[i] for i in range(5)], 0)
    rest = jnp.concatenate([total[5 + i][:, :over] for i in range(4)] + [last], 0)
    tail = jnp.concatenate([total[8][:, over : over + 16]] * 5, 0)
    both = jnp.concatenate([wide, rest], 1)
    first = jnp.concatenate([both[:, :owned], tail], 1)
    second = jnp.concatenate([both[:, owned:], tail], 1)
    mine = place_ref[1] == 0
    kept_ref[...] = jnp.where(mine, first, second)
    sent_ref[...] = jnp.where(mine, second, first)


def split_up(place, pieces, owned):
    shape = jax.ShapeDtypeStruct((HALF, owned + 16), F32)
    return pl.pallas_call(
        split_kernel,
        out_shape=(shape, shape),
        in_specs=[SMEM, VMEM],
        out_specs=(VMEM, VMEM),
        compiler_params=PARAMS,
        name="split_up",
    )(place, pieces)


def finish_kernel(place_ref, kept_ref, came_ref, inverse_ref, up_ref):
    owned = up_ref.shape[1]
    kept, came = kept_ref[...], came_ref[...]
    high, low = kept[:1, owned : owned + 1], kept[:1, owned + 1 : owned + 2]
    inv_root = lax.rsqrt(32.0 * high + low)
    mine = place_ref[1] == 0
    total = jnp.concatenate([jnp.where(mine, kept, came), jnp.where(mine, came, kept)], 0)
    up = lax.dot_general(
        inverse_ref[...],
        total,
        (((1,), (0,)), ((), ())),
        precision=lax.Precision.HIGHEST,
        preferred_element_type=F32,
    )
    up_ref[...] = (inv_root * up)[:, :owned]


def finish_up(place, kept, came, inverse, owned):
    return pl.pallas_call(
        finish_kernel,
        out_shape=jax.ShapeDtypeStruct((K, owned), F32),
        in_specs=[SMEM] + [VMEM] * 3,
        out_specs=VMEM,
        compiler_params=PARAMS,
        name="finish_up",
    )(place, kept, came, inverse)


def both_halves(first, own, other):
    return jnp.where(
        first, jnp.concatenate([own, other], 0), jnp.concatenate([other, own], 0)
    )


def aligned(block):
    return jnp.pad(block, ((0, 0), (0, 128 - block.shape[1])))


def local(tokens, out_grads, test_matrix, slot_counts):
    spots = jnp.stack([lax.axis_index(("z", "x", "c")), lax.axis_index("c")])
    place = jnp.concatenate([spots, slot_counts, sibling(slot_counts)])
    scale = LIVE ** -0.5
    width = tokens.shape[1] // 64

    kept, sent, grads = load_and_sketch(spots, test_matrix.T, out_grads)
    sketch_part = jnp.concatenate([kept, sibling(sent)], 1)
    other_tokens, sketch_part = lax.optimization_barrier((sibling(tokens), sketch_part))
    sent_grads, sketch_part = lax.optimization_barrier((out_grads, sketch_part))
    other_grads = sibling(sent_grads)
    other_tokens = hold(other_tokens)

    ranged = chips_sum(
        token_part(place, y_pieces(sketch_part), tokens, other_tokens, 1.0), scale
    )
    back_part = feature_part(ranged, tokens, other_tokens)
    other_grads, back_part = lax.optimization_barrier((other_grads, back_part))
    back = y_pieces(back_part)
    other_grads = hold(other_grads)
    transposed = chips_sum(
        token_part(place, back, grads, other_grads, D ** -0.5), scale, ("x", "z")
    )
    again = y_pieces(feature_part(transposed, grads, other_grads))
    whole_range = chips_sum(
        token_part(place, again, tokens, other_tokens, FF ** -0.5), scale
    )

    other_range = sibling(whole_range)
    both = jnp.concatenate([whole_range, other_range], 0)
    gram_part = dot(both, both, ((1,), (1,)))
    gram_part = jnp.concatenate([gram_part[:HALF], gram_part[HALF:, HALF:]], 1)
    high = gram_part.astype(BF16)
    low = (gram_part - high.astype(F32)).astype(BF16)
    projected = feature_part(whole_range, tokens, other_tokens)
    joined = y_pieces(jnp.concatenate([projected, aligned(high), aligned(low)], 1))

    up, gram_rows = up_part(place, joined, grads, other_grads)
    up_pieces = exchange(up, ("x", "z"))
    gram_rows, place = lax.optimization_barrier((gram_rows, place))
    own_rows, corner = gram_rows[:, :K], gram_rows[:, K : K + HALF]
    other_rows = jnp.concatenate([own_rows[:, HALF:].T, corner], 1)
    gram = jnp.concatenate([own_rows, other_rows], 0)
    first = place[1] == 0
    gram = jnp.where(first, gram, jnp.roll(gram, (HALF, HALF), (0, 1)))
    lower = jnp.linalg.cholesky(gram)
    inverse = lax.linalg.triangular_solve(
        lower, jnp.eye(K, dtype=F32), left_side=True, lower=True
    )

    owned = out_grads.shape[1] // 64
    kept_up, sent_up = split_up(place, up_pieces, owned)
    adapter_up = finish_up(place, kept_up, sibling(sent_up), inverse, owned).T

    own = both_halves(first, whole_range, other_range)
    own = lax.dynamic_slice_in_dim(own, place[0] * width, width, 1).astype(F32)
    adapter_down = jnp.dot(inverse, own, precision=lax.Precision.HIGHEST).T * D ** 0.5
    return adapter_down, adapter_up


def solution(mesh):
    split = Mesh(mesh.devices.reshape(8, 4, 2, 4), ("z", "x", "c", "y"))
    dp = ("z", "x", "c")
    placed = (P(dp, "y"), P(dp, "y"), P("y", None), P(dp))
    return jax.shard_map(
        local,
        mesh=split,
        in_specs=placed,
        out_specs=(P(("y",) + dp, None), P(("y",) + dp, None)),
        check_vma=False,
    )
```

```python
import functools

import jax
import jax.numpy as jnp
from jax import lax
from jax.experimental import pallas as pl
from jax.experimental.pallas import tpu as pltpu
from jax.sharding import Mesh, PartitionSpec as P

D = 8192
FF = 28672
K = 80
HALF = K // 2
LIVE = 16384
F32 = jnp.float32
BF16 = jnp.bfloat16
CHUNKS = 14
BLOCK = 1024
HOLDS = 8
VMEM = pl.BlockSpec(memory_space=pltpu.VMEM)
SMEM = pl.BlockSpec(memory_space=pltpu.SMEM)
PARAMS = pltpu.CompilerParams(vmem_limit_bytes=16 << 20)


def dot(left, right, contract):
    return lax.dot_general(left, right, (contract, ((), ())), preferred_element_type=F32)


def shifted(value, axis, size, step):
    return lax.ppermute(value, axis, [(i, (i + step) % size) for i in range(size)])


def sibling(value):
    return shifted(value, "c", 2, 1)


def y_pieces(sent):
    return [sent] + [shifted(sent, "y", 4, step) for step in (3, 2, 1)]


def to_tiles(array):
    rows, cols = array.shape
    tiles = array.reshape(rows // 8, 8, cols // 128, 128).transpose(0, 2, 1, 3)
    return tiles.reshape(-1, 8, 128)


def from_tiles(tiles, rows, cols):
    split = tiles.reshape(rows // 8, cols // 128, 8, 128).transpose(0, 2, 1, 3)
    return split.reshape(rows, cols)


def exchange(pieces, axes):
    return lax.all_to_all(pieces, axes, 0, 0, tiled=True)


def spread(piece, axes, count):
    return exchange(jnp.broadcast_to(piece[None], (count,) + piece.shape), axes)


def chips_sum(part, scale, axes=("z", "x")):
    rows, cols = part.shape
    tiles = to_tiles(part)
    count = tiles.shape[0]
    per = -(-count // 32)
    tiles = jnp.pad(tiles, ((0, 32 * per - count), (0, 0), (0, 0)))
    pieces = tiles.reshape(32, per, 8, 128)
    mine = (exchange(pieces, axes).astype(F32).sum(0) * scale).astype(BF16)
    whole = spread(mine, axes, 32).reshape(32 * per, 8, 128)[:count]
    return from_tiles(whole, rows, cols)


def cost(big):
    rows, cols = big.shape
    return pl.CostEstimate(
        flops=4 * HALF * rows * cols, bytes_accessed=4 * rows * cols, transcendentals=0
    )


def in_vmem(array):
    return pltpu.with_memory_space_constraint(array, pltpu.VMEM)


def hold_kernel(given_ref, held_ref, sems):
    rows = given_ref.shape[0] // HOLDS
    copies = []
    for k in range(HOLDS):
        part = pl.ds(k * rows, rows)
        copy = pltpu.make_async_copy(given_ref.at[part], held_ref.at[part], sems.at[k])
        copy.start()
        copies.append(copy)
    for copy in copies:
        copy.wait()


def hold(given):
    given = pltpu.with_memory_space_constraint(given, pltpu.HBM)
    return pl.pallas_call(
        hold_kernel,
        out_shape=pltpu.VMEM(given.shape, given.dtype),
        in_specs=[pl.BlockSpec(memory_space=pl.ANY)],
        out_specs=VMEM,
        scratch_shapes=[pltpu.SemaphoreType.DMA((HOLDS,))],
        compiler_params=PARAMS,
        cost_estimate=pl.CostEstimate(
            flops=0, bytes_accessed=4 * given.size, transcendentals=0
        ),
        name="hold",
    )(given)


def load_kernel(
    place_ref, test_ref, grads_ref, kept_ref, sent_ref, held_ref, test_held, sems, test_sems
):
    width = grads_ref.shape[1] // CHUNKS
    copies = []
    for k in range(CHUNKS):
        cols = pl.ds(k * width, width)
        first = pltpu.make_async_copy(
            test_ref.at[:, cols], test_held.at[:, cols], test_sems.at[k]
        )
        second = pltpu.make_async_copy(
            grads_ref.at[:, cols], held_ref.at[:, cols], sems.at[k]
        )
        first.start()
        second.start()
        copies.append((first, second))
    total = None
    for k in range(CHUNKS):
        cols = pl.ds(k * width, width)
        copies[k][0].wait()
        copies[k][1].wait()
        step = dot(test_held[:, cols], held_ref[:, cols], ((1,), (1,)))
        total = step if total is None else total + step
    first = place_ref[1] == 0
    kept_ref[...] = jnp.where(first, total[:HALF], total[HALF:]).astype(BF16)
    sent_ref[...] = jnp.where(first, total[HALF:], total[:HALF]).astype(BF16)


def load_and_sketch(place, test_t, grads):
    rows, cols = grads.shape
    test_t = pltpu.with_memory_space_constraint(test_t, pltpu.HBM)
    grads = pltpu.with_memory_space_constraint(grads, pltpu.HBM)
    part = jax.ShapeDtypeStruct((HALF, rows), BF16)
    return pl.pallas_call(
        load_kernel,
        out_shape=(part, part, pltpu.VMEM((rows, cols), BF16)),
        in_specs=[SMEM] + [pl.BlockSpec(memory_space=pl.ANY)] * 2,
        out_specs=(VMEM,) * 3,
        scratch_shapes=[
            pltpu.VMEM((K, cols), BF16),
            pltpu.SemaphoreType.DMA((CHUNKS,)),
            pltpu.SemaphoreType.DMA((CHUNKS,)),
        ],
        compiler_params=PARAMS,
        cost_estimate=cost(grads),
        name="load_and_sketch",
    )(place, test_t, grads)


def summed_small(place_ref, refs, scale):
    total = refs[0][...].astype(F32)
    for ref in refs[1:]:
        total = total + ref[...].astype(F32)
    rows = total.shape[1] // 2
    slot = lax.broadcasted_iota(jnp.int32, total.shape, 1)
    own = slot < place_ref[2]
    other = (slot >= rows) & (slot < place_ref[3] + rows)
    return jnp.where(own | other, total * scale, 0.0).astype(BF16)


def token_kernel(scale, place_ref, *refs):
    own_ref, other_ref, part_ref = refs[-3:]
    small = summed_small(place_ref, refs[:-3], scale)
    rows = own_ref.shape[0]
    for k in range(own_ref.shape[1] // BLOCK):
        cols = slice(k * BLOCK, (k + 1) * BLOCK)
        out = dot(small[:, :rows], own_ref[:, cols], ((1,), (0,)))
        out = out + dot(small[:, rows:], other_ref[:, cols], ((1,), (0,)))
        part_ref[:, cols] = out.astype(BF16)


def token_part(place, pieces, own, other, scale):
    return pl.pallas_call(
        functools.partial(token_kernel, scale),
        out_shape=jax.ShapeDtypeStruct((HALF, own.shape[1]), BF16),
        in_specs=[SMEM] + [VMEM] * (len(pieces) + 2),
        out_specs=VMEM,
        compiler_params=PARAMS,
        cost_estimate=cost(own),
        name="token_part",
    )(place, *pieces, in_vmem(own), in_vmem(other))


def feature_kernel(small_ref, own_ref, other_ref, part_ref):
    rows = own_ref.shape[0]
    for at, big_ref in ((0, own_ref), (rows, other_ref)):
        total = None
        for k in range(big_ref.shape[1] // BLOCK):
            cols = slice(k * BLOCK, (k + 1) * BLOCK)
            step = dot(small_ref[:, cols], big_ref[:, cols], ((1,), (1,)))
            total = step if total is None else total + step
        part_ref[:, at : at + rows] = total.astype(BF16)


def feature_part(small, own, other):
    return pl.pallas_call(
        feature_kernel,
        out_shape=jax.ShapeDtypeStruct((HALF, 2 * own.shape[0]), BF16),
        in_specs=[VMEM] * 3,
        out_specs=VMEM,
        compiler_params=PARAMS,
        cost_estimate=cost(own),
        name="feature_part",
    )(small, in_vmem(own), in_vmem(other))


def up_kernel(place_ref, *refs):
    own_ref, other_ref, part_ref, gram_ref = refs[-4:]
    rows = own_ref.shape[0]
    pieces = [ref.at[:, : 2 * rows] for ref in refs[:-4]]
    small = summed_small(place_ref, pieces, 1.0)
    gram = None
    for ref in refs[:-4]:
        high = ref[:, 2 * rows : 2 * rows + 128].astype(F32)
        low = ref[:, 2 * rows + 128 : 2 * rows + 256].astype(F32)
        gram = high + low if gram is None else gram + (high + low)
    spot = lax.broadcasted_iota(jnp.int32, gram.shape, 1)
    gram_ref[...] = jnp.where(spot == K + HALF, place_ref[1].astype(F32), gram)
    width = own_ref.shape[1] // 32
    over = width - 128
    lane = lax.broadcasted_iota(jnp.int32, (8, 128 - over), 1)
    high = (place_ref[2] // 32 + place_ref[3] // 32).astype(F32)
    low = (place_ref[2] % 32 + place_ref[3] % 32).astype(F32)
    digits = jnp.where(lane == 0, high, jnp.where(lane == 1, low, 0.0))
    for z in range(8):
        cols = slice(4 * z * width, 4 * (z + 1) * width)
        out = dot(small[:, :rows], own_ref[:, cols], ((1,), (0,)))
        out = out + dot(small[:, rows:], other_ref[:, cols], ((1,), (0,)))
        for x in range(4):
            piece = out[:, x * width : (x + 1) * width]
            rest = piece[:, 128:]
            last = rest[32:]
            beside = [last[:, 32 * i : 32 * i + 32] for i in range(3)] + [digits]
            for i in range(5):
                part_ref[8 * x + z, i] = piece[8 * i : 8 * i + 8, :128].astype(BF16)
            for i in range(4):
                tile = jnp.concatenate([rest[8 * i : 8 * i + 8], beside[i]], 1)
                part_ref[8 * x + z, 5 + i] = tile.astype(BF16)


def up_part(place, pieces, own, other):
    return pl.pallas_call(
        up_kernel,
        out_shape=(
            jax.ShapeDtypeStruct((32, 9, 8, 128), BF16),
            jax.ShapeDtypeStruct((HALF, 128), F32),
        ),
        in_specs=[SMEM] + [VMEM] * (len(pieces) + 2),
        out_specs=(VMEM, VMEM),
        compiler_params=PARAMS,
        cost_estimate=cost(own),
        name="up_part",
    )(place, *pieces, in_vmem(own), in_vmem(other))


def split_kernel(place_ref, pieces_ref, kept_ref, sent_ref):
    owned = kept_ref.shape[1] - 16
    total = pieces_ref[0].astype(F32)
    for k in range(1, pieces_ref.shape[0]):
        total = total + pieces_ref[k].astype(F32)
    over = 2 * owned - 128
    last = jnp.concatenate([total[5 + i][:, over:] for i in range(3)], 1)
    wide = jnp.concatenate([total[i] for i in range(5)], 0)
    rest = jnp.concatenate([total[5 + i][:, :over] for i in range(4)] + [last], 0)
    tail = jnp.concatenate([total[8][:, over : over + 16]] * 5, 0)
    both = jnp.concatenate([wide, rest], 1)
    first = jnp.concatenate([both[:, :owned], tail], 1)
    second = jnp.concatenate([both[:, owned:], tail], 1)
    mine = place_ref[1] == 0
    kept_ref[...] = jnp.where(mine, first, second)
    sent_ref[...] = jnp.where(mine, second, first)


def split_up(place, pieces, owned):
    shape = jax.ShapeDtypeStruct((HALF, owned + 16), F32)
    return pl.pallas_call(
        split_kernel,
        out_shape=(shape, shape),
        in_specs=[SMEM, VMEM],
        out_specs=(VMEM, VMEM),
        compiler_params=PARAMS,
        name="split_up",
    )(place, pieces)


def finish_kernel(place_ref, kept_ref, came_ref, inverse_ref, up_ref):
    owned = up_ref.shape[1]
    kept, came = kept_ref[...], came_ref[...]
    high, low = kept[:1, owned : owned + 1], kept[:1, owned + 1 : owned + 2]
    inv_root = lax.rsqrt(32.0 * high + low)
    mine = place_ref[1] == 0
    total = jnp.concatenate([jnp.where(mine, kept, came), jnp.where(mine, came, kept)], 0)
    up = lax.dot_general(
        inverse_ref[...],
        total,
        (((1,), (0,)), ((), ())),
        precision=lax.Precision.HIGHEST,
        preferred_element_type=F32,
    )
    up_ref[...] = (inv_root * up)[:, :owned]


def finish_up(place, kept, came, inverse, owned):
    return pl.pallas_call(
        finish_kernel,
        out_shape=jax.ShapeDtypeStruct((K, owned), F32),
        in_specs=[SMEM] + [VMEM] * 3,
        out_specs=VMEM,
        compiler_params=PARAMS,
        name="finish_up",
    )(place, kept, came, inverse)


def both_halves(first, own, other):
    return jnp.where(
        first, jnp.concatenate([own, other], 0), jnp.concatenate([other, own], 0)
    )


def aligned(block):
    return jnp.pad(block, ((0, 0), (0, 128 - block.shape[1])))


def local(tokens, out_grads, test_matrix, slot_counts):
    spots = jnp.stack([lax.axis_index(("z", "x", "c")), lax.axis_index("c")])
    place = jnp.concatenate([spots, slot_counts, sibling(slot_counts)])
    scale = LIVE ** -0.5
    width = tokens.shape[1] // 64

    kept, sent, grads = load_and_sketch(spots, test_matrix.T, out_grads)
    sketch_part = jnp.concatenate([kept, sibling(sent)], 1)
    other_tokens, sketch_part = lax.optimization_barrier((sibling(tokens), sketch_part))
    sent_grads, sketch_part = lax.optimization_barrier((out_grads, sketch_part))
    other_grads = sibling(sent_grads)
    other_tokens = hold(other_tokens)

    ranged = chips_sum(
        token_part(place, y_pieces(sketch_part), tokens, other_tokens, 1.0), scale
    )
    back_part = feature_part(ranged, tokens, other_tokens)
    other_grads, back_part = lax.optimization_barrier((other_grads, back_part))
    back = y_pieces(back_part)
    other_grads = hold(other_grads)
    transposed = chips_sum(
        token_part(place, back, grads, other_grads, D ** -0.5), scale, ("x", "z")
    )
    again = y_pieces(feature_part(transposed, grads, other_grads))
    whole_range = chips_sum(
        token_part(place, again, tokens, other_tokens, FF ** -0.5), scale
    )

    other_range = sibling(whole_range)
    both = jnp.concatenate([whole_range, other_range], 0)
    gram_part = dot(both, both, ((1,), (1,)))
    gram_part = jnp.concatenate([gram_part[:HALF], gram_part[HALF:, HALF:]], 1)
    high = gram_part.astype(BF16)
    low = (gram_part - high.astype(F32)).astype(BF16)
    projected = feature_part(whole_range, tokens, other_tokens)
    joined = y_pieces(jnp.concatenate([projected, aligned(high), aligned(low)], 1))

    up, gram_rows = up_part(place, joined, grads, other_grads)
    up_pieces = exchange(up, ("x", "z"))
    own_rows, corner = gram_rows[:, :K], gram_rows[:, K : K + HALF]
    other_rows = jnp.concatenate([own_rows[:, HALF:].T, corner], 1)
    gram = jnp.concatenate([own_rows, other_rows], 0)
    first = gram_rows[:1, K + HALF : K + HALF + 1] == 0.0
    gram = jnp.where(first, gram, jnp.roll(gram, (HALF, HALF), (0, 1)))
    lower = jnp.linalg.cholesky(gram)
    inverse = lax.linalg.triangular_solve(
        lower, jnp.eye(K, dtype=F32), left_side=True, lower=True
    )

    owned = out_grads.shape[1] // 64
    kept_up, sent_up = split_up(place, up_pieces, owned)
    adapter_up = finish_up(place, kept_up, sibling(sent_up), inverse, owned).T

    inverse, spots = lax.optimization_barrier((inverse, place))
    own = both_halves(first, whole_range, other_range)
    own = lax.dynamic_slice_in_dim(own, spots[0] * width, width, 1).astype(F32)
    adapter_down = jnp.dot(inverse, own, precision=lax.Precision.HIGHEST).T * D ** 0.5
    return adapter_down, adapter_up


def solution(mesh):
    split = Mesh(mesh.devices.reshape(8, 4, 2, 4), ("z", "x", "c", "y"))
    dp = ("z", "x", "c")
    placed = (P(dp, "y"), P(dp, "y"), P("y", None), P(dp))
    return jax.shard_map(
        local,
        mesh=split,
        in_specs=placed,
        out_specs=(P(("y",) + dp, None), P(("y",) + dp, None)),
        check_vma=False,
    )
```
